32 devices in a mesh: facet: 8 (over z, x), uv: 4 (over y, core).
Axes of the slice: x: 2, y: 2, z: 4, core: 2. Of those that a mesh axis runs over, the one named last changes fastest.
Arguments:
- sky_image: bfloat16 [128, 16384], P('uv', 'facet'), may hold values from -6 to 6
- subgrid_offsets: int32 [8], replicated, may hold values from 0 to 2047
- owner_order: int32 [8], replicated, may hold values from 0 to 7, each once
- visibility_count: int32 [8], P('facet'), may hold values from 1 to 512, 2048 in all
- visibility_cell: int32 [8, 512], P('facet'), may hold values from 0 to 255
- observed: bfloat16 [8, 2, 128, 512], P('facet', None, 'uv'), may hold values from -6 to 6
- visibility_weight: float32 [8, 128, 512], P('facet', 'uv'), may hold values from 0.3 to 3
- row_kernel: float32 [7], replicated, may hold values from 0.3 to 1
- column_kernel: float32 [7], replicated, may hold values from 0.3 to 1
Outputs:
- weighted_residual: float32 [8, 2, 128, 512], P('facet', None, 'uv')
- dirty_image: float32 [128, 16384], P('uv', 'facet')
The draws below stay inside these ranges and needn't reach their ends.
Inputs may be any that keep to these rules, and one draw needn't show every extreme that they name: `owner_order`: a permutation of the 8 subgrids over the slots. `visibility_count`: the counts sum to 2048, and some slot has exactly 512 live visibilities in every draw.
All inputs are finite; a program needn't handle non-finite values. No bound on the sum of `visibility_count` on one device may be relied on, other than what follows from the above.
Results may differ from the reference program's by a relative error of at most 0.022.
Values may be sent and summed in bfloat16 or wider, within the bound.
A program may use at most 64 MiB of HBM per device.

```python
import math
import jax
import jax.numpy as jnp
import numpy as np
from jax import lax

FR = 2048
XC = 128
SG = 256
TAPS = 7
VMAX = 512
NSUB = 8
NROWS = 16384
COLS = 128
N_FACET = 8


def place_ends(values, stream_key, least, largest):
    longest = values.shape.index(max(values.shape))
    spots = []
    for shift in (0, 1):
        where = [jax.random.randint(jax.random.fold_in(stream_key, axis), (), 0, length) for axis, length in enumerate(values.shape)]
        where[longest] = (where[longest] + shift) % values.shape[longest]
        spots.append(tuple(where))
    return values.at[spots[0]].set(least).at[spots[1]].set(largest)


def steps_of(key, dims, cuts, low, high):
    factor_of = 1.0
    for axis_at, shards_of in cuts:
        heights = jax.random.uniform(jax.random.fold_in(jax.random.fold_in(key, 6), axis_at), (shards_of,), jnp.float32, low / len(cuts), high / len(cuts))
        factor_of = factor_of * jnp.repeat(jnp.exp(heights), dims[axis_at] // shards_of).reshape((-1,) + (1,) * (len(dims) - 1 - axis_at))
    return factor_of


def length_profile(number_of, total, limit, lean):
    weights = [(1 << 20) // math.isqrt(standing ** lean) + 1 for standing in range(2, number_of + 1)]
    spare, given = total - limit - (number_of - 1), [1] * (number_of - 1)
    while spare > 0:
        candidates = [i for i in range(number_of - 1) if given[i] < limit]
        pool, left = sum([weights[i] for i in candidates]), spare
        for i in candidates:
            addition = min(limit - given[i], max(1, left * weights[i] // pool), spare)
            given[i] = given[i] + addition
            spare = spare - addition
    return np.array([limit] + given)


def uneven_parts(own_key, count, total, reach, skew):
    if count == 2:
        one = jax.random.randint(own_key, (), max(1, total - reach), min(reach, total - 1) + 1)
        return jnp.stack([one, total - one])
    tallies = jnp.asarray(length_profile(count, total, reach, skew), jnp.int32)
    couples = (count - 1) // 2
    source_of, sink = tallies[1:1 + 2 * couples:2], tallies[2:2 + 2 * couples:2]
    slack = jnp.minimum(source_of - 1, reach - sink)
    moved = jax.random.randint(jax.random.fold_in(own_key, 1), (couples,), 0, 1 << 20) % (slack + 1)
    tallies = tallies.at[1:1 + 2 * couples:2].set(source_of - moved).at[2:2 + 2 * couples:2].set(sink + moved)
    return tallies[jax.random.permutation(jax.random.fold_in(own_key, 2), count)]


def bell_draw(own_key, dims, width, bound, cuts=(), kind=jnp.bfloat16):
    array = jax.random.normal(own_key, dims, jnp.float32) * width
    if len(cuts) > 0:
        array = steps_of(own_key, dims, cuts, -0.22, 0.18) * array
    return jnp.clip(array, min=-bound, max=bound).astype(kind)


def setup_inputs(seed: int = 0) -> dict:
    splits = jax.random.split(jax.random.key(seed), 10)
    return {
        "sky_image": bell_draw(splits[0], (COLS, NROWS), 1.0, 6.0, ((0, 4), (1, 8))),
        "subgrid_offsets": place_ends(jax.random.randint(splits[1], (NSUB,), 0, FR), jax.random.fold_in(splits[1], 1), 0, FR - 1).astype(jnp.int32),
        "owner_order": jax.random.permutation(splits[2], NSUB).astype(jnp.int32),
        "visibility_count": uneven_parts(splits[3], NSUB, NSUB * VMAX // 2, VMAX, 2).astype(jnp.int32),
        "visibility_cell": place_ends(jax.random.randint(splits[4], (NSUB, VMAX), 0, SG), jax.random.fold_in(splits[4], 1), 0, SG - 1).astype(jnp.int32),
        "observed": bell_draw(splits[5], (NSUB, 2, COLS, VMAX), 1.0, 6.0, ((0, 8), (2, 4))),
        "visibility_weight": jnp.clip(jnp.exp(math.log(3.0) - 2.3025851 * jax.random.uniform(splits[6], (NSUB, COLS, VMAX), jnp.float32) ** steps_of(splits[6], (NSUB, COLS, VMAX), ((0, 8), (1, 4)), -0.2, 0.2)), 0.3, 3.0),
        "row_kernel": jnp.clip(jax.random.uniform(splits[7], (TAPS,), jnp.float32, 0.3, 1.0), 0.3, 1.0),
        "column_kernel": jnp.clip(jax.random.uniform(splits[8], (TAPS,), jnp.float32, 0.3, 1.0), 0.3, 1.0),
    }


def taper_values(strip_rows):
    position = jnp.arange(strip_rows, dtype=jnp.float32)
    return jnp.sin((position + 0.5) * (math.pi / strip_rows)) / math.sqrt(strip_rows)

def shift_values(slot_offsets, strip_rows):
    position = jnp.arange(strip_rows, dtype=jnp.int32)
    shifted = jnp.bitwise_and(slot_offsets[:, None] * position[None, :], strip_rows - 1)
    angle_shift = shifted.astype(jnp.float32) * (2.0 * math.pi / strip_rows)
    return jnp.stack([jnp.cos(angle_shift), -jnp.sin(angle_shift)], axis=1)

def base_tables(coarse, strip_rows):
    position = jnp.arange(strip_rows, dtype=jnp.int32)
    base = jnp.bitwise_and(jnp.arange(coarse, dtype=jnp.int32)[:, None] * position[None, :], strip_rows - 1)
    angle_base = base.astype(jnp.float32) * (2.0 * math.pi / strip_rows)
    cosine = jnp.cos(angle_base)
    sine_part = jnp.sin(angle_base)
    upper = jnp.stack([cosine, sine_part])
    lower = jnp.stack([-sine_part, cosine])
    return jnp.stack([upper, lower]).astype(jnp.bfloat16)

def expand_tables(facet, coarse, strip_rows, facet_count):
    grid_width = 2 * coarse
    image_rows = strip_rows * facet_count
    fine_index = jnp.arange(grid_width, dtype=jnp.int32)[:, None]
    coarse_index = jnp.arange(coarse, dtype=jnp.int32)[None, :]
    centre = (facet * strip_rows + strip_rows // 2)[..., None, None]
    product = jnp.bitwise_and(jnp.bitwise_and(fine_index * coarse_index, grid_width - 1) * (image_rows // grid_width) + (fine_index - 2 * coarse_index) * centre, image_rows - 1)
    radians = product.astype(jnp.float32) * (2.0 * math.pi / image_rows)
    factor = 1.0 / math.sqrt(facet_count * coarse)
    cosine = jnp.cos(radians) * factor
    sine_part = jnp.sin(radians) * factor
    upper = jnp.stack([cosine, -sine_part], axis=-3)
    lower = jnp.stack([sine_part, cosine], axis=-3)
    return jnp.stack([upper, lower], axis=-4).astype(jnp.bfloat16)

def degrid_matrix(positions, kernel, grid_width):
    margin = (kernel.shape[0] - 1) // 2
    distance = jnp.arange(grid_width, dtype=jnp.int32)[None, :] - positions[:, None] + margin
    matrix = jnp.zeros(distance.shape, jnp.float32)
    for tap_index in range(kernel.shape[0]):
        matrix = matrix + jnp.where(distance == tap_index, kernel[tap_index], 0.0)
    return matrix.astype(jnp.bfloat16)

def convolve(padded, kernel, columns, flipped):
    tap_count = kernel.shape[0]
    result = jnp.zeros(padded.shape[:-2] + (columns, padded.shape[-1]), jnp.float32)
    for tap_index in range(tap_count):
        first_column = tap_count - 1 - tap_index if flipped else tap_index
        result = result + kernel[tap_index] * padded[..., first_column:first_column + columns, :]
    return result

def rounded(values):
    return lax.optimization_barrier(values.astype(jnp.bfloat16)).astype(jnp.float32)

def reference(sky_image, subgrid_offsets, owner_order, visibility_count, visibility_cell, observed, visibility_weight, row_kernel, column_kernel):
    strip_rows = FR
    columns = sky_image.shape[0]
    margin = (TAPS - 1) // 2
    window_taper = taper_values(strip_rows)
    windowed = (sky_image.astype(jnp.float32).reshape(columns, N_FACET, strip_rows) * window_taper[None, None, :]).astype(jnp.bfloat16)
    windowed_wide = windowed.astype(jnp.float32)
    expansion = expand_tables(jnp.arange(N_FACET, dtype=jnp.int32), XC, strip_rows, N_FACET).astype(jnp.float32)
    base_table = base_tables(XC, strip_rows).astype(jnp.float32)
    slot_offset = subgrid_offsets[owner_order]
    shift_table = shift_values(slot_offset, strip_rows)
    row_index = jnp.arange(VMAX, dtype=jnp.int32)

    def one_slot(dirty_sum, inputs):
        shift, live_count, positions, observed_slot, weights = inputs
        modulated = rounded(shift[:, None, None, :] * windowed_wide[None, :, :, :])
        contribution = rounded(jnp.einsum('pqkr,qcfr->fpck', base_table, modulated))
        subgrid = jnp.einsum('fpqjk,fqck->pcj', expansion, contribution)
        padded = jnp.pad(subgrid, ((0, 0), (margin, margin), (0, 0)))
        grid_values = rounded(convolve(padded, column_kernel, columns, False))
        degrid_table = degrid_matrix(positions, row_kernel, SG).astype(jnp.float32)
        model_rows = jnp.einsum('vj,pcj->pcv', degrid_table, grid_values)
        live_rows = (row_index < live_count).astype(jnp.float32)
        residual = live_rows[None, None, :] * weights[None, :, :] * (observed_slot.astype(jnp.float32) - model_rows)
        gridded = jnp.einsum('vj,pcv->pcj', degrid_table, rounded(residual))
        padded_back = jnp.pad(gridded, ((0, 0), (margin, margin), (0, 0)))
        back_grid = rounded(convolve(padded_back, column_kernel, columns, True))
        back_pieces = rounded(jnp.einsum('fqpjk,qcj->fpck', expansion, back_grid))
        back_rows = jnp.einsum('pqkr,fpck->qcfr', base_table, back_pieces)
        dirty_sum = dirty_sum + lax.optimization_barrier(jnp.sum(shift[:, None, None, :] * back_rows, axis=0))
        return (dirty_sum, residual)
    dirty_sum, residuals = lax.scan(one_slot, jnp.zeros((columns, N_FACET, strip_rows), jnp.float32), (shift_table, visibility_count, visibility_cell, observed, visibility_weight))
    dirty_image = (dirty_sum * window_taper[None, None, :]).reshape(columns, N_FACET * strip_rows)
    return (residuals, dirty_image)
```

```python
import functools
import math

import jax
import jax.numpy as jnp
from jax import lax
from jax.experimental import pallas as pl
from jax.experimental.pallas import tpu as pltpu
from jax.sharding import PartitionSpec as P

XC = 128
SG = 256
LANES = 128
EDGE = 8
NT = (((1,), (1,)), ((), ()))
F32 = jnp.float32
BF16 = jnp.bfloat16


def sine(a):
    square = a * a
    total = jnp.full_like(a, 1.0 / math.factorial(17))
    for order in range(15, 0, -2):
        sign = -1.0 if order % 4 == 3 else 1.0
        total = total * square + sign / math.factorial(order)
    return a * total


def cosine(a):
    square = a * a
    total = jnp.full_like(a, -1.0 / math.factorial(18))
    for order in range(16, -1, -2):
        sign = -1.0 if order % 4 == 2 else 1.0
        total = total * square + sign / math.factorial(order)
    return total


def turn(steps, period):
    steps = jnp.bitwise_and(steps, period - 1)
    steps = jnp.where(steps >= period // 2, steps - period, steps)
    angle = steps.astype(F32) * (2.0 * math.pi / period)
    return cosine(angle), sine(angle)


def iota(shape, dim):
    return lax.broadcasted_iota(jnp.int32, shape, dim)


def kernel(
    facets, bands, offsets, owner, count, rowk, colk, cell, sky_hbm, obs_hbm, wt_hbm,
    res_hbm, dirty,
    sky, obs, wt, obs_halo, wt_halo, taper, shift, windowed, table, total,
    send1, recv1, grid, z, z_halo, residual, send2, recv2,
    local_sem, send_sem1, recv_sem1, send_sem2, recv_sem2, halo_send, halo_recv,
):
    me = lax.axis_index("facet")
    band = lax.axis_index("uv")
    right, left = lax.rem(band + 1, bands), lax.rem(band + bands - 1, bands)
    columns, strip = sky.shape
    slots = facets
    blocks = strip // LANES
    taps = colk.shape[0]
    margin = (taps - 1) // 2
    live_slots = cell.shape[1]

    sky_copy = pltpu.make_async_copy(sky_hbm, sky, local_sem.at[0])
    obs_copy = pltpu.make_async_copy(obs_hbm.at[0], obs, local_sem.at[1])
    wt_copy = pltpu.make_async_copy(wt_hbm.at[0], wt, local_sem.at[2])
    sky_copy.start()
    obs_copy.start()
    wt_copy.start()

    barrier = pltpu.get_barrier_semaphore()

    def greet(d, carry):
        pl.semaphore_signal(
            barrier, inc=1, device_id={"facet": lax.rem(me + d, facets)},
            device_id_type=pl.DeviceIdType.MESH,
        )
        return carry

    lax.fori_loop(1, facets, greet, 0)
    for side in (left, right):
        pl.semaphore_signal(
            barrier, inc=1, device_id={"uv": side}, device_id_type=pl.DeviceIdType.MESH
        )

    def exchange(index, src, dst, side):
        return pltpu.make_async_remote_copy(
            src_ref=src, dst_ref=dst, send_sem=halo_send.at[index],
            recv_sem=halo_recv.at[index], device_id={"uv": side},
            device_id_type=pl.DeviceIdType.MESH,
        )

    def out1(d):
        to = lax.rem(me + d, facets)
        return pltpu.make_async_remote_copy(
            src_ref=send1.at[to], dst_ref=recv1.at[me], send_sem=send_sem1.at[to],
            recv_sem=recv_sem1.at[me], device_id={"facet": to},
            device_id_type=pl.DeviceIdType.MESH,
        )

    def in1(d):
        source = lax.rem(me + facets - d, facets)
        return pltpu.make_async_remote_copy(
            src_ref=send1.at[source], dst_ref=recv1.at[source], send_sem=send_sem1.at[source],
            recv_sem=recv_sem1.at[source], device_id={"facet": source},
            device_id_type=pl.DeviceIdType.MESH,
        )

    def out2(d):
        to = lax.rem(me + d, facets)
        return pltpu.make_async_remote_copy(
            src_ref=send2.at[to], dst_ref=recv2.at[me], send_sem=send_sem2.at[to],
            recv_sem=recv_sem2.at[me], device_id={"facet": to},
            device_id_type=pl.DeviceIdType.MESH,
        )

    def in2(d):
        source = lax.rem(me + facets - d, facets)
        return pltpu.make_async_remote_copy(
            src_ref=send2.at[source], dst_ref=recv2.at[source], send_sem=send_sem2.at[source],
            recv_sem=recv_sem2.at[source], device_id={"facet": source},
            device_id_type=pl.DeviceIdType.MESH,
        )

    def each(action):
        def step(d, carry):
            action(d)
            return carry

        lax.fori_loop(1, facets, step, 0)

    position = iota((1, strip), 1)
    taper[...] = sine((position.astype(F32) + 0.5) * (math.pi / strip)) * (1.0 / math.sqrt(strip))
    offset = jnp.zeros((slots, strip), jnp.int32)
    slot_row = iota((slots, strip), 0)
    for i in range(slots):
        offset = jnp.where(slot_row == i, offsets[owner[i]], offset)
    shift_cos, shift_sin = turn(offset * iota((slots, strip), 1), strip)
    shift[0] = shift_cos
    shift[1] = -shift_sin
    frequency = iota((XC, LANES), 0)
    first = (2 * me + 1) * (strip // facets)
    start = turn(frequency * (iota((XC, LANES), 1) + first), strip)
    step_cos, step_sin = turn(frequency * LANES, strip)
    sky_copy.wait()
    windowed[...] = (sky[...].astype(F32) * taper[...]).astype(BF16).astype(F32)
    total[...] = jnp.zeros_like(total)

    def contribute(block, carry):
        c, s = carry
        upper = jnp.concatenate([c, s], axis=1)
        lower = jnp.concatenate([-s, c], axis=1)
        base = jnp.concatenate([upper, lower], axis=0).astype(BF16)
        table[block] = base
        rows = pl.ds(pl.multiple_of(block * LANES, LANES), LANES)
        piece = windowed[:, rows]
        real, imag = shift[0, :, rows], shift[1, :, rows]
        modulated = jnp.concatenate(
            [
                jnp.concatenate([real[i : i + 1] * piece, imag[i : i + 1] * piece], axis=1)
                for i in range(slots)
            ],
            axis=0,
        ).astype(BF16)
        total[...] += lax.dot_general(modulated, base, NT, preferred_element_type=F32)
        return c * step_cos - s * step_sin, s * step_cos + c * step_sin

    lax.fori_loop(0, blocks, contribute, start)
    send1[...] = total[...].astype(BF16).reshape(send1.shape)

    pl.semaphore_wait(barrier, facets + 1)
    each(lambda d: out1(d).start())
    recv1[me] = send1[me]
    early = [
        exchange(0, obs_hbm.at[0, :, pl.ds(columns - 2 * EDGE, 2 * EDGE)], obs_halo.at[0], right),
        exchange(1, obs_hbm.at[0, :, pl.ds(0, 2 * EDGE)], obs_halo.at[1], left),
        exchange(2, wt_hbm.at[0, pl.ds(columns - EDGE, EDGE)], wt_halo.at[0], right),
        exchange(3, wt_hbm.at[0, pl.ds(0, EDGE)], wt_halo.at[1], left),
    ]
    for copy in early:
        copy.start()

    factor = 1.0 / math.sqrt(facets * XC)
    fine_cos, fine_sin = turn(iota((SG, SG), 0) * iota((SG, SG), 1), SG)
    fine_cos = (fine_cos * factor).astype(BF16)
    fine_sin = (fine_sin * factor).astype(BF16)
    distance = iota((SG, live_slots), 0) - cell[...] + margin
    degrid = jnp.zeros((SG, live_slots), F32)
    for t in range(taps):
        degrid = jnp.where(distance == t, rowk[t], degrid)
    degrid = degrid.astype(BF16)
    grid_cos = jnp.dot(fine_cos, degrid, preferred_element_type=F32)
    grid_sin = jnp.dot(fine_sin, degrid, preferred_element_type=F32)
    grid[0:SG, 0:live_slots] = grid_cos.astype(BF16)
    grid[0:SG, live_slots:] = grid_sin.astype(BF16)
    grid[SG:, 0:live_slots] = (-grid_sin).astype(BF16)
    grid[SG:, live_slots:] = grid_cos.astype(BF16)

    each(lambda d: in1(d).wait_recv())
    blank = jnp.zeros((columns, SG - XC), F32)
    sums = [jnp.zeros((columns, SG), F32), jnp.zeros((columns, SG), F32)]
    for f in range(facets):
        place = (2 * f + 1) * (SG // (2 * facets)) % SG
        arrived = recv1[f].astype(F32)
        for q in range(2):
            wide = jnp.concatenate([arrived[:, q * XC : (q + 1) * XC], blank], axis=1)
            sums[q] = sums[q] + pltpu.roll(wide, place, 1)
    z[...] = jnp.concatenate(sums, axis=1)
    late = [
        exchange(4, z.at[pl.ds(columns - EDGE, EDGE)], z_halo.at[0], right),
        exchange(5, z.at[pl.ds(0, EDGE)], z_halo.at[1], left),
    ]
    for copy in late:
        copy.start()

    obs_copy.wait()
    wt_copy.wait()
    for copy in early:
        copy.wait_recv()
    for copy in late:
        copy.wait_recv()
    rows = columns + 2 * EDGE
    before = jnp.where(band == 0, 0.0, z_halo[0])
    after = jnp.where(band == bands - 1, 0.0, z_halo[1])
    padded = jnp.concatenate([before, z[...], after], axis=0)
    convolved = jnp.zeros_like(padded)
    for t in range(taps):
        convolved = convolved + colk[t] * pltpu.roll(padded, (margin - t) % rows, 0)
    model = jnp.dot(convolved.astype(BF16), grid[...], preferred_element_type=F32)
    row = iota((rows, live_slots), 0)
    lowest = jnp.where(band == 0, EDGE, EDGE - margin)
    highest = jnp.where(band == bands - 1, EDGE + columns, EDGE + columns + margin)
    valid = (row >= lowest) & (row < highest) & (iota((rows, live_slots), 1) < count[0])
    weight = jnp.where(valid, jnp.concatenate([wt_halo[0], wt[...], wt_halo[1]], axis=0), 0.0)
    parts = []
    for p in range(2):
        seen = jnp.concatenate(
            [
                obs_halo[0, p].astype(F32)[EDGE:],
                obs[p].astype(F32),
                obs_halo[1, p].astype(F32)[:EDGE],
            ],
            axis=0,
        )
        parts.append(weight * (seen - model[:, p * live_slots : (p + 1) * live_slots]))
        residual[p] = parts[p][EDGE : EDGE + columns]
    res_copy = pltpu.make_async_copy(residual, res_hbm.at[0], local_sem.at[3])
    res_copy.start()
    rounded = jnp.concatenate(parts, axis=1).astype(BF16)
    gridded = lax.dot_general(rounded, grid[...], NT, preferred_element_type=F32)
    back = jnp.zeros_like(gridded)
    for t in range(taps):
        back = back + colk[t] * pltpu.roll(gridded, (t - margin) % rows, 0)
    back = back[EDGE : EDGE + columns]
    for f in range(facets):
        place = (2 * f + 1) * (SG // (2 * facets)) % SG
        send2[f] = jnp.concatenate(
            [
                pltpu.roll(back[:, p * SG : (p + 1) * SG], (SG - place) % SG, 1)[:, :XC]
                for p in range(2)
            ],
            axis=1,
        ).astype(BF16)
    each(lambda d: out2(d).start())
    recv2[me] = send2[me]
    for copy in early + late:
        copy.wait_send()
    each(lambda d: out1(d).wait_send())
    each(lambda d: in2(d).wait_recv())

    pieces = recv2[...].reshape(slots * columns, 2 * XC)

    def image(block, carry):
        rows = pl.ds(pl.multiple_of(block * LANES, LANES), LANES)
        back_rows = jnp.dot(pieces, table[block], preferred_element_type=F32)
        real, imag = shift[0, :, rows], shift[1, :, rows]
        strip_sum = jnp.zeros((columns, LANES), F32)
        for i in range(slots):
            own = back_rows[i * columns : (i + 1) * columns]
            strip_sum = strip_sum + real[i : i + 1] * own[:, :LANES] + imag[i : i + 1] * own[:, LANES:]
        dirty[:, rows] = strip_sum * taper[:, rows]
        return carry

    lax.fori_loop(0, blocks, image, 0)
    res_copy.wait()
    each(lambda d: out2(d).wait_send())


def local(
    sky_image, subgrid_offsets, owner_order, visibility_count, visibility_cell, observed,
    visibility_weight, row_kernel, column_kernel,
):
    facets, bands = lax.axis_size("facet"), lax.axis_size("uv")
    columns, strip = sky_image.shape
    slots = facets
    live_slots = visibility_cell.shape[1]
    smem, vmem = pl.BlockSpec(memory_space=pltpu.SMEM), pl.BlockSpec(memory_space=pltpu.VMEM)
    hbm = pl.BlockSpec(memory_space=pl.ANY)
    dma = pltpu.SemaphoreType.DMA
    traded = pltpu.VMEM((facets, columns, 2 * XC), BF16)
    return pl.pallas_call(
        functools.partial(kernel, facets, bands),
        out_shape=(
            jax.ShapeDtypeStruct(observed.shape, F32),
            jax.ShapeDtypeStruct(sky_image.shape, F32),
        ),
        in_specs=[smem, smem, smem, smem, smem, vmem, hbm, hbm, hbm],
        out_specs=(hbm, vmem),
        scratch_shapes=[
            pltpu.VMEM((columns, strip), BF16),
            pltpu.VMEM((2, columns, live_slots), BF16),
            pltpu.VMEM((columns, live_slots), F32),
            pltpu.VMEM((2, 2, 2 * EDGE, live_slots), BF16),
            pltpu.VMEM((2, EDGE, live_slots), F32),
            pltpu.VMEM((1, strip), F32),
            pltpu.VMEM((2, slots, strip), F32),
            pltpu.VMEM((columns, strip), F32),
            pltpu.VMEM((strip // LANES, 2 * XC, 2 * LANES), BF16),
            pltpu.VMEM((slots * columns, 2 * XC), F32),
            traded,
            traded,
            pltpu.VMEM((2 * SG, 2 * live_slots), BF16),
            pltpu.VMEM((columns, 2 * SG), F32),
            pltpu.VMEM((2, EDGE, 2 * SG), F32),
            pltpu.VMEM((2, columns, live_slots), F32),
            traded,
            traded,
            dma((4,)),
            dma((facets,)),
            dma((facets,)),
            dma((facets,)),
            dma((facets,)),
            dma((6,)),
            dma((6,)),
        ],
        compiler_params=pltpu.CompilerParams(
            collective_id=0, has_side_effects=True, vmem_limit_bytes=32 * 1024 * 1024
        ),
    )(
        subgrid_offsets, owner_order, visibility_count, row_kernel, column_kernel,
        visibility_cell, sky_image, observed, visibility_weight,
    )


def solution(mesh):
    in_specs = (
        P("uv", "facet"), P(), P(), P("facet"), P("facet", None), P("facet", None, "uv", None),
        P("facet", "uv", None), P(), P(),
    )
    out_specs = (P("facet", None, "uv", None), P("uv", "facet"))
    return jax.shard_map(local, mesh=mesh, in_specs=in_specs, out_specs=out_specs, check_vma=False)
```

```python
import functools
import math

import jax
import jax.numpy as jnp
from jax import lax
from jax.experimental import pallas as pl
from jax.experimental.pallas import tpu as pltpu
from jax.sharding import PartitionSpec as P

XC = 128
SG = 256
LANES = 128
EDGE = 8
GROUP = 4
NT = (((1,), (1,)), ((), ()))
F32 = jnp.float32
BF16 = jnp.bfloat16


def sine(a):
    square = a * a
    total = jnp.full_like(a, 1.0 / math.factorial(17))
    for order in range(15, 0, -2):
        sign = -1.0 if order % 4 == 3 else 1.0
        total = total * square + sign / math.factorial(order)
    return a * total


def cosine(a):
    square = a * a
    total = jnp.full_like(a, -1.0 / math.factorial(18))
    for order in range(16, -1, -2):
        sign = -1.0 if order % 4 == 2 else 1.0
        total = total * square + sign / math.factorial(order)
    return total


def turn(steps, period):
    steps = jnp.bitwise_and(steps, period - 1)
    steps = jnp.where(steps >= period // 2, steps - period, steps)
    angle = steps.astype(F32) * (2.0 * math.pi / period)
    return cosine(angle), sine(angle)


def iota(shape, dim):
    return lax.broadcasted_iota(jnp.int32, shape, dim)


def kernel(
    facets, bands, offsets_hbm, owner_hbm, count_hbm, rowk_hbm, colk_hbm, cell_hbm,
    sky_hbm, obs_hbm, wt_hbm,
    res_hbm, dirty,
    offsets, owner, count, rowk, colk, cell, sky, obs, wt, obs_halo, wt_halo, taper, shift, windowed, table, total,
    send1, recv1, grid, z, z_halo, residual, send2, recv2,
    local_sem, send_sem1, recv_sem1, send_sem2, recv_sem2, halo_send, halo_recv,
):
    me = lax.axis_index("facet")
    band = lax.axis_index("uv")
    right, left = lax.rem(band + 1, bands), lax.rem(band + bands - 1, bands)
    columns, strip = sky.shape
    slots = facets
    blocks = strip // LANES
    taps = colk.shape[0]
    margin = (taps - 1) // 2
    live_slots = cell.shape[1]

    sky_copy = pltpu.make_async_copy(sky_hbm, sky, local_sem.at[0])
    obs_copy = pltpu.make_async_copy(obs_hbm.at[0], obs, local_sem.at[1])
    wt_copy = pltpu.make_async_copy(wt_hbm.at[0], wt, local_sem.at[2])
    small = [
        pltpu.make_async_copy(source, target, local_sem.at[4 + i])
        for i, (source, target) in enumerate(
            [
                (offsets_hbm, offsets), (owner_hbm, owner), (count_hbm, count),
                (rowk_hbm, rowk), (colk_hbm, colk), (cell_hbm, cell),
            ]
        )
    ]
    sky_copy.start()
    for copy in small:
        copy.start()
    obs_copy.start()
    wt_copy.start()

    barrier = pltpu.get_barrier_semaphore()

    def greet(d, carry):
        pl.semaphore_signal(
            barrier, inc=1, device_id={"facet": lax.rem(me + d, facets)},
            device_id_type=pl.DeviceIdType.MESH,
        )
        return carry

    lax.fori_loop(1, facets, greet, 0)
    for side in (left, right):
        pl.semaphore_signal(
            barrier, inc=1, device_id={"uv": side}, device_id_type=pl.DeviceIdType.MESH
        )

    def exchange(index, src, dst, side):
        return pltpu.make_async_remote_copy(
            src_ref=src, dst_ref=dst, send_sem=halo_send.at[index],
            recv_sem=halo_recv.at[index], device_id={"uv": side},
            device_id_type=pl.DeviceIdType.MESH,
        )

    def out1(d):
        to = lax.rem(me + d, facets)
        return pltpu.make_async_remote_copy(
            src_ref=send1.at[to], dst_ref=recv1.at[me], send_sem=send_sem1.at[to],
            recv_sem=recv_sem1.at[me], device_id={"facet": to},
            device_id_type=pl.DeviceIdType.MESH,
        )

    def in1(d):
        source = lax.rem(me + facets - d, facets)
        return pltpu.make_async_remote_copy(
            src_ref=send1.at[source], dst_ref=recv1.at[source], send_sem=send_sem1.at[source],
            recv_sem=recv_sem1.at[source], device_id={"facet": source},
            device_id_type=pl.DeviceIdType.MESH,
        )

    def out2(d):
        to = lax.rem(me + d, facets)
        return pltpu.make_async_remote_copy(
            src_ref=send2.at[to], dst_ref=recv2.at[me], send_sem=send_sem2.at[to],
            recv_sem=recv_sem2.at[me], device_id={"facet": to},
            device_id_type=pl.DeviceIdType.MESH,
        )

    def in2(d):
        source = lax.rem(me + facets - d, facets)
        return pltpu.make_async_remote_copy(
            src_ref=send2.at[source], dst_ref=recv2.at[source], send_sem=send_sem2.at[source],
            recv_sem=recv_sem2.at[source], device_id={"facet": source},
            device_id_type=pl.DeviceIdType.MESH,
        )

    def each(action):
        def step(d, carry):
            action(d)
            return carry

        lax.fori_loop(1, facets, step, 0)

    position = iota((1, strip), 1)
    taper[...] = sine((position.astype(F32) + 0.5) * (math.pi / strip)) * (1.0 / math.sqrt(strip))
    frequency = iota((XC, LANES), 0)
    first = (2 * me + 1) * (strip // facets)
    start = turn(frequency * (iota((XC, LANES), 1) + first), strip)
    step_cos, step_sin = turn(frequency * LANES, strip)
    for copy in small:
        copy.wait()
    offset = jnp.zeros((slots, strip), jnp.int32)
    slot_row = iota((slots, strip), 0)
    for i in range(slots):
        offset = jnp.where(slot_row == i, offsets[owner[i]], offset)
    shift_cos, shift_sin = turn(offset * iota((slots, strip), 1), strip)
    shift[0] = shift_cos
    shift[1] = -shift_sin
    sky_copy.wait()
    windowed[...] = (sky[...].astype(F32) * taper[...]).astype(BF16).astype(F32)
    total[...] = jnp.zeros_like(total)

    def contribute(group, carry):
        c, s = carry
        bases, pieces = [], []
        for member in range(GROUP):
            block = group * GROUP + member
            upper = jnp.concatenate([c, s], axis=1)
            lower = jnp.concatenate([-s, c], axis=1)
            base = jnp.concatenate([upper, lower], axis=0).astype(BF16)
            table[block] = base
            bases.append(base)
            rows = pl.ds(pl.multiple_of(block * LANES, LANES), LANES)
            piece = windowed[:, rows]
            real, imag = shift[0, :, rows], shift[1, :, rows]
            pieces.append(
                jnp.concatenate(
                    [
                        jnp.concatenate(
                            [real[i : i + 1] * piece, imag[i : i + 1] * piece], axis=1
                        ).astype(BF16)
                        for i in range(slots)
                    ],
                    axis=0,
                )
            )
            c, s = c * step_cos - s * step_sin, s * step_cos + c * step_sin
        total[...] += lax.dot_general(
            jnp.concatenate(pieces, axis=1), jnp.concatenate(bases, axis=1), NT,
            preferred_element_type=F32,
        )
        return c, s

    lax.fori_loop(0, blocks // GROUP, contribute, start)
    send1[...] = total[...].astype(BF16).reshape(send1.shape)

    pl.semaphore_wait(barrier, facets + 1)
    each(lambda d: out1(d).start())
    recv1[me] = send1[me]
    early = [
        exchange(0, obs_hbm.at[0, :, pl.ds(columns - 2 * EDGE, 2 * EDGE)], obs_halo.at[0], right),
        exchange(1, obs_hbm.at[0, :, pl.ds(0, 2 * EDGE)], obs_halo.at[1], left),
        exchange(2, wt_hbm.at[0, pl.ds(columns - EDGE, EDGE)], wt_halo.at[0], right),
        exchange(3, wt_hbm.at[0, pl.ds(0, EDGE)], wt_halo.at[1], left),
    ]
    for copy in early:
        copy.start()

    factor = 1.0 / math.sqrt(facets * XC)
    fine_cos, fine_sin = turn(iota((SG, SG), 0) * iota((SG, SG), 1), SG)
    fine_cos = (fine_cos * factor).astype(BF16)
    fine_sin = (fine_sin * factor).astype(BF16)
    distance = iota((SG, live_slots), 0) - cell[...] + margin
    degrid = jnp.zeros((SG, live_slots), F32)
    for t in range(taps):
        degrid = jnp.where(distance == t, rowk[t], degrid)
    degrid = degrid.astype(BF16)
    grid_cos = jnp.dot(fine_cos, degrid, preferred_element_type=F32)
    grid_sin = jnp.dot(fine_sin, degrid, preferred_element_type=F32)
    grid[0:SG, 0:live_slots] = grid_cos.astype(BF16)
    grid[0:SG, live_slots:] = grid_sin.astype(BF16)
    grid[SG:, 0:live_slots] = (-grid_sin).astype(BF16)
    grid[SG:, live_slots:] = grid_cos.astype(BF16)

    each(lambda d: in1(d).wait_recv())
    blank = jnp.zeros((columns, SG - XC), F32)
    sums = [jnp.zeros((columns, SG), F32), jnp.zeros((columns, SG), F32)]
    for f in range(facets):
        place = (2 * f + 1) * (SG // (2 * facets)) % SG
        arrived = recv1[f].astype(F32)
        for q in range(2):
            wide = jnp.concatenate([arrived[:, q * XC : (q + 1) * XC], blank], axis=1)
            sums[q] = sums[q] + pltpu.roll(wide, place, 1)
    z[...] = jnp.concatenate(sums, axis=1)
    late = [
        exchange(4, z.at[pl.ds(columns - EDGE, EDGE)], z_halo.at[0], right),
        exchange(5, z.at[pl.ds(0, EDGE)], z_halo.at[1], left),
    ]
    for copy in late:
        copy.start()

    obs_copy.wait()
    wt_copy.wait()
    for copy in early:
        copy.wait_recv()
    for copy in late:
        copy.wait_recv()
    rows = columns + 2 * EDGE
    before = jnp.where(band == 0, 0.0, z_halo[0])
    after = jnp.where(band == bands - 1, 0.0, z_halo[1])
    padded = jnp.concatenate([before, z[...], after], axis=0)
    convolved = jnp.zeros_like(padded)
    for t in range(taps):
        convolved = convolved + colk[t] * pltpu.roll(padded, (margin - t) % rows, 0)
    model = jnp.dot(convolved.astype(BF16), grid[...], preferred_element_type=F32)
    row = iota((rows, live_slots), 0)
    lowest = jnp.where(band == 0, EDGE, EDGE - margin)
    highest = jnp.where(band == bands - 1, EDGE + columns, EDGE + columns + margin)
    valid = (row >= lowest) & (row < highest) & (iota((rows, live_slots), 1) < count[0])
    weight = jnp.where(valid, jnp.concatenate([wt_halo[0], wt[...], wt_halo[1]], axis=0), 0.0)
    parts = []
    for p in range(2):
        seen = jnp.concatenate(
            [
                obs_halo[0, p].astype(F32)[EDGE:],
                obs[p].astype(F32),
                obs_halo[1, p].astype(F32)[:EDGE],
            ],
            axis=0,
        )
        parts.append(weight * (seen - model[:, p * live_slots : (p + 1) * live_slots]))
        residual[p] = parts[p][EDGE : EDGE + columns]
    res_copy = pltpu.make_async_copy(residual, res_hbm.at[0], local_sem.at[3])
    res_copy.start()
    rounded = jnp.concatenate(parts, axis=1).astype(BF16)
    gridded = lax.dot_general(rounded, grid[...], NT, preferred_element_type=F32)
    back = jnp.zeros_like(gridded)
    for t in range(taps):
        back = back + colk[t] * pltpu.roll(gridded, (t - margin) % rows, 0)
    back = back[EDGE : EDGE + columns]
    for f in range(facets):
        place = (2 * f + 1) * (SG // (2 * facets)) % SG
        send2[f] = jnp.concatenate(
            [
                pltpu.roll(back[:, p * SG : (p + 1) * SG], (SG - place) % SG, 1)[:, :XC]
                for p in range(2)
            ],
            axis=1,
        ).astype(BF16)
    each(lambda d: out2(d).start())
    recv2[me] = send2[me]
    for copy in early + late:
        copy.wait_send()
    each(lambda d: out1(d).wait_send())
    each(lambda d: in2(d).wait_recv())

    pieces = recv2[...].reshape(slots * columns, 2 * XC)

    def image(block, carry):
        rows = pl.ds(pl.multiple_of(block * LANES, LANES), LANES)
        back_rows = jnp.dot(pieces, table[block], preferred_element_type=F32)
        real, imag = shift[0, :, rows], shift[1, :, rows]
        strip_sum = jnp.zeros((columns, LANES), F32)
        for i in range(slots):
            own = back_rows[i * columns : (i + 1) * columns]
            strip_sum = strip_sum + real[i : i + 1] * own[:, :LANES] + imag[i : i + 1] * own[:, LANES:]
        dirty[:, rows] = strip_sum * taper[:, rows]
        return carry

    lax.fori_loop(0, blocks, image, 0, unroll=GROUP)
    res_copy.wait()
    each(lambda d: out2(d).wait_send())


def local(
    sky_image, subgrid_offsets, owner_order, visibility_count, visibility_cell, observed,
    visibility_weight, row_kernel, column_kernel,
):
    facets, bands = lax.axis_size("facet"), lax.axis_size("uv")
    columns, strip = sky_image.shape
    slots = facets
    live_slots = visibility_cell.shape[1]
    vmem = pl.BlockSpec(memory_space=pltpu.VMEM)
    hbm = pl.BlockSpec(memory_space=pltpu.HBM)
    dma = pltpu.SemaphoreType.DMA
    traded = pltpu.VMEM((facets, columns, 2 * XC), BF16)
    return pl.pallas_call(
        functools.partial(kernel, facets, bands),
        out_shape=(
            jax.ShapeDtypeStruct(observed.shape, F32),
            jax.ShapeDtypeStruct(sky_image.shape, F32),
        ),
        in_specs=[hbm] * 9,
        out_specs=(hbm, vmem),
        scratch_shapes=[
            pltpu.SMEM(subgrid_offsets.shape, jnp.int32),
            pltpu.SMEM(owner_order.shape, jnp.int32),
            pltpu.SMEM(visibility_count.shape, jnp.int32),
            pltpu.SMEM(row_kernel.shape, F32),
            pltpu.SMEM(column_kernel.shape, F32),
            pltpu.VMEM(visibility_cell.shape, jnp.int32),
            pltpu.VMEM((columns, strip), BF16),
            pltpu.VMEM((2, columns, live_slots), BF16),
            pltpu.VMEM((columns, live_slots), F32),
            pltpu.VMEM((2, 2, 2 * EDGE, live_slots), BF16),
            pltpu.VMEM((2, EDGE, live_slots), F32),
            pltpu.VMEM((1, strip), F32),
            pltpu.VMEM((2, slots, strip), F32),
            pltpu.VMEM((columns, strip), F32),
            pltpu.VMEM((strip // LANES, 2 * XC, 2 * LANES), BF16),
            pltpu.VMEM((slots * columns, 2 * XC), F32),
            traded,
            traded,
            pltpu.VMEM((2 * SG, 2 * live_slots), BF16),
            pltpu.VMEM((columns, 2 * SG), F32),
            pltpu.VMEM((2, EDGE, 2 * SG), F32),
            pltpu.VMEM((2, columns, live_slots), F32),
            traded,
            traded,
            dma((10,)),
            dma((facets,)),
            dma((facets,)),
            dma((facets,)),
            dma((facets,)),
            dma((6,)),
            dma((6,)),
        ],
        compiler_params=pltpu.CompilerParams(
            collective_id=0, has_side_effects=True, vmem_limit_bytes=63 * 1024 * 1024
        ),
    )(
        subgrid_offsets, owner_order, visibility_count, row_kernel, column_kernel,
        visibility_cell, sky_image, observed, visibility_weight,
    )


def solution(mesh):
    in_specs = (
        P("uv", "facet"), P(), P(), P("facet"), P("facet", None), P("facet", None, "uv", None),
        P("facet", "uv", None), P(), P(),
    )
    out_specs = (P("facet", None, "uv", None), P("uv", "facet"))
    return jax.shard_map(local, mesh=mesh, in_specs=in_specs, out_specs=out_specs, check_vma=False)
```

```python
import functools
import math

import jax
import jax.numpy as jnp
from jax import lax
from jax.experimental import pallas as pl
from jax.experimental.pallas import tpu as pltpu
from jax.sharding import PartitionSpec as P

XC = 128
SG = 256
LANES = 128
EDGE = 8
GROUP = 4
NT = (((1,), (1,)), ((), ()))
F32 = jnp.float32
BF16 = jnp.bfloat16


def sine(a):
    square = a * a
    total = jnp.full_like(a, 1.0 / math.factorial(17))
    for order in range(15, 0, -2):
        sign = -1.0 if order % 4 == 3 else 1.0
        total = total * square + sign / math.factorial(order)
    return a * total


def cosine(a):
    square = a * a
    total = jnp.full_like(a, -1.0 / math.factorial(18))
    for order in range(16, -1, -2):
        sign = -1.0 if order % 4 == 2 else 1.0
        total = total * square + sign / math.factorial(order)
    return total


def turn(steps, period):
    steps = jnp.bitwise_and(steps, period - 1)
    steps = jnp.where(steps >= period // 2, steps - period, steps)
    angle = steps.astype(F32) * (2.0 * math.pi / period)
    return cosine(angle), sine(angle)


def iota(shape, dim):
    return lax.broadcasted_iota(jnp.int32, shape, dim)


def kernel(
    facets, bands, offsets_hbm, owner_hbm, count_hbm, rowk_hbm, colk_hbm, cell_hbm,
    sky_hbm, obs_hbm, wt_hbm,
    residual, collected, table, shift, taper,
    offsets, owner, count, rowk, colk, cell, sky, obs, wt, obs_halo, wt_halo, windowed, total,
    send1, recv1, grid, z, z_halo, send2, recv2,
    local_sem, send_sem1, recv_sem1, send_sem2, recv_sem2, halo_send, halo_recv,
):
    me = lax.axis_index("facet")
    band = lax.axis_index("uv")
    right, left = lax.rem(band + 1, bands), lax.rem(band + bands - 1, bands)
    columns, strip = sky.shape
    slots = facets
    blocks = strip // LANES
    taps = colk.shape[0]
    margin = (taps - 1) // 2
    live_slots = cell.shape[1]

    sky_copy = pltpu.make_async_copy(sky_hbm, sky, local_sem.at[0])
    obs_copy = pltpu.make_async_copy(obs_hbm.at[0], obs, local_sem.at[1])
    wt_copy = pltpu.make_async_copy(wt_hbm.at[0], wt, local_sem.at[2])
    small = [
        pltpu.make_async_copy(source, target, local_sem.at[4 + i])
        for i, (source, target) in enumerate(
            [
                (offsets_hbm, offsets), (owner_hbm, owner), (count_hbm, count),
                (rowk_hbm, rowk), (colk_hbm, colk), (cell_hbm, cell),
            ]
        )
    ]
    sky_copy.start()
    for copy in small:
        copy.start()
    obs_copy.start()
    wt_copy.start()

    barrier = pltpu.get_barrier_semaphore()

    def greet(d, carry):
        pl.semaphore_signal(
            barrier, inc=1, device_id={"facet": lax.rem(me + d, facets)},
            device_id_type=pl.DeviceIdType.MESH,
        )
        return carry

    lax.fori_loop(1, facets, greet, 0)
    for side in (left, right):
        pl.semaphore_signal(
            barrier, inc=1, device_id={"uv": side}, device_id_type=pl.DeviceIdType.MESH
        )

    def exchange(index, src, dst, side):
        return pltpu.make_async_remote_copy(
            src_ref=src, dst_ref=dst, send_sem=halo_send.at[index],
            recv_sem=halo_recv.at[index], device_id={"uv": side},
            device_id_type=pl.DeviceIdType.MESH,
        )

    def out1(d):
        to = lax.rem(me + d, facets)
        return pltpu.make_async_remote_copy(
            src_ref=send1.at[to], dst_ref=recv1.at[me], send_sem=send_sem1.at[to],
            recv_sem=recv_sem1.at[me], device_id={"facet": to},
            device_id_type=pl.DeviceIdType.MESH,
        )

    def in1(d):
        source = lax.rem(me + facets - d, facets)
        return pltpu.make_async_remote_copy(
            src_ref=send1.at[source], dst_ref=recv1.at[source], send_sem=send_sem1.at[source],
            recv_sem=recv_sem1.at[source], device_id={"facet": source},
            device_id_type=pl.DeviceIdType.MESH,
        )

    def out2(d):
        to = lax.rem(me + d, facets)
        return pltpu.make_async_remote_copy(
            src_ref=send2.at[to], dst_ref=recv2.at[me], send_sem=send_sem2.at[to],
            recv_sem=recv_sem2.at[me], device_id={"facet": to},
            device_id_type=pl.DeviceIdType.MESH,
        )

    def in2(d):
        source = lax.rem(me + facets - d, facets)
        return pltpu.make_async_remote_copy(
            src_ref=send2.at[source], dst_ref=recv2.at[source], send_sem=send_sem2.at[source],
            recv_sem=recv_sem2.at[source], device_id={"facet": source},
            device_id_type=pl.DeviceIdType.MESH,
        )

    def each(action):
        def step(d, carry):
            action(d)
            return carry

        lax.fori_loop(1, facets, step, 0)

    position = iota((1, strip), 1)
    taper[...] = sine((position.astype(F32) + 0.5) * (math.pi / strip)) * (1.0 / math.sqrt(strip))
    frequency = iota((XC, LANES), 0)
    first = (2 * me + 1) * (strip // facets)
    start = turn(frequency * (iota((XC, LANES), 1) + first), strip)
    step_cos, step_sin = turn(frequency * LANES, strip)
    for copy in small:
        copy.wait()
    offset = jnp.zeros((slots, strip), jnp.int32)
    slot_row = iota((slots, strip), 0)
    for i in range(slots):
        offset = jnp.where(slot_row == i, offsets[owner[i]], offset)
    shift_cos, shift_sin = turn(offset * iota((slots, strip), 1), strip)
    shift[0] = shift_cos
    shift[1] = -shift_sin
    sky_copy.wait()
    windowed[...] = (sky[...].astype(F32) * taper[...]).astype(BF16).astype(F32)
    total[...] = jnp.zeros_like(total)

    def contribute(group, carry):
        c, s = carry
        bases, pieces = [], []
        for member in range(GROUP):
            block = group * GROUP + member
            upper = jnp.concatenate([c, s], axis=1)
            lower = jnp.concatenate([-s, c], axis=1)
            base = jnp.concatenate([upper, lower], axis=0).astype(BF16)
            table[block] = base
            bases.append(base)
            rows = pl.ds(pl.multiple_of(block * LANES, LANES), LANES)
            piece = windowed[:, rows]
            real, imag = shift[0, :, rows], shift[1, :, rows]
            pieces.append(
                jnp.concatenate(
                    [
                        jnp.concatenate(
                            [real[i : i + 1] * piece, imag[i : i + 1] * piece], axis=1
                        ).astype(BF16)
                        for i in range(slots)
                    ],
                    axis=0,
                )
            )
            c, s = c * step_cos - s * step_sin, s * step_cos + c * step_sin
        total[...] += lax.dot_general(
            jnp.concatenate(pieces, axis=1), jnp.concatenate(bases, axis=1), NT,
            preferred_element_type=F32,
        )
        return c, s

    lax.fori_loop(0, blocks // GROUP, contribute, start)
    send1[...] = total[...].astype(BF16).reshape(send1.shape)

    pl.semaphore_wait(barrier, facets + 1)
    each(lambda d: out1(d).start())
    recv1[me] = send1[me]
    early = [
        exchange(0, obs_hbm.at[0, :, pl.ds(columns - 2 * EDGE, 2 * EDGE)], obs_halo.at[0], right),
        exchange(1, obs_hbm.at[0, :, pl.ds(0, 2 * EDGE)], obs_halo.at[1], left),
        exchange(2, wt_hbm.at[0, pl.ds(columns - EDGE, EDGE)], wt_halo.at[0], right),
        exchange(3, wt_hbm.at[0, pl.ds(0, EDGE)], wt_halo.at[1], left),
    ]
    for copy in early:
        copy.start()

    factor = 1.0 / math.sqrt(facets * XC)
    fine_cos, fine_sin = turn(iota((SG, SG), 0) * iota((SG, SG), 1), SG)
    fine_cos = (fine_cos * factor).astype(BF16)
    fine_sin = (fine_sin * factor).astype(BF16)
    distance = iota((SG, live_slots), 0) - cell[...] + margin
    degrid = jnp.zeros((SG, live_slots), F32)
    for t in range(taps):
        degrid = jnp.where(distance == t, rowk[t], degrid)
    degrid = degrid.astype(BF16)
    grid_cos = jnp.dot(fine_cos, degrid, preferred_element_type=F32)
    grid_sin = jnp.dot(fine_sin, degrid, preferred_element_type=F32)
    grid[0:SG, 0:live_slots] = grid_cos.astype(BF16)
    grid[0:SG, live_slots:] = grid_sin.astype(BF16)
    grid[SG:, 0:live_slots] = (-grid_sin).astype(BF16)
    grid[SG:, live_slots:] = grid_cos.astype(BF16)

    each(lambda d: in1(d).wait_recv())
    blank = jnp.zeros((columns, SG - XC), F32)
    sums = [jnp.zeros((columns, SG), F32), jnp.zeros((columns, SG), F32)]
    for f in range(facets):
        place = (2 * f + 1) * (SG // (2 * facets)) % SG
        arrived = recv1[f].astype(F32)
        for q in range(2):
            wide = jnp.concatenate([arrived[:, q * XC : (q + 1) * XC], blank], axis=1)
            sums[q] = sums[q] + pltpu.roll(wide, place, 1)
    z[...] = jnp.concatenate(sums, axis=1)
    late = [
        exchange(4, z.at[pl.ds(columns - EDGE, EDGE)], z_halo.at[0], right),
        exchange(5, z.at[pl.ds(0, EDGE)], z_halo.at[1], left),
    ]
    for copy in late:
        copy.start()

    obs_copy.wait()
    wt_copy.wait()
    for copy in early:
        copy.wait_recv()
    for copy in late:
        copy.wait_recv()
    rows = columns + 2 * EDGE
    before = jnp.where(band == 0, 0.0, z_halo[0])
    after = jnp.where(band == bands - 1, 0.0, z_halo[1])
    padded = jnp.concatenate([before, z[...], after], axis=0)
    convolved = jnp.zeros_like(padded)
    for t in range(taps):
        convolved = convolved + colk[t] * pltpu.roll(padded, (margin - t) % rows, 0)
    model = jnp.dot(convolved.astype(BF16), grid[...], preferred_element_type=F32)
    row = iota((rows, live_slots), 0)
    lowest = jnp.where(band == 0, EDGE, EDGE - margin)
    highest = jnp.where(band == bands - 1, EDGE + columns, EDGE + columns + margin)
    valid = (row >= lowest) & (row < highest) & (iota((rows, live_slots), 1) < count[0])
    weight = jnp.where(valid, jnp.concatenate([wt_halo[0], wt[...], wt_halo[1]], axis=0), 0.0)
    parts = []
    for p in range(2):
        seen = jnp.concatenate(
            [
                obs_halo[0, p].astype(F32)[EDGE:],
                obs[p].astype(F32),
                obs_halo[1, p].astype(F32)[:EDGE],
            ],
            axis=0,
        )
        parts.append(weight * (seen - model[:, p * live_slots : (p + 1) * live_slots]))
        residual[0, p] = parts[p][EDGE : EDGE + columns]
    rounded = jnp.concatenate(parts, axis=1).astype(BF16)
    gridded = lax.dot_general(rounded, grid[...], NT, preferred_element_type=F32)
    back = jnp.zeros_like(gridded)
    for t in range(taps):
        back = back + colk[t] * pltpu.roll(gridded, (t - margin) % rows, 0)
    back = back[EDGE : EDGE + columns]
    for f in range(facets):
        place = (2 * f + 1) * (SG // (2 * facets)) % SG
        send2[f] = jnp.concatenate(
            [
                pltpu.roll(back[:, p * SG : (p + 1) * SG], (SG - place) % SG, 1)[:, :XC]
                for p in range(2)
            ],
            axis=1,
        ).astype(BF16)
    each(lambda d: out2(d).start())
    recv2[me] = send2[me]
    for copy in early + late:
        copy.wait_send()
    each(lambda d: out1(d).wait_send())
    each(lambda d: in2(d).wait_recv())

    collected[...] = recv2[...]
    each(lambda d: out2(d).wait_send())


def image_kernel(
    residual, collected, table, shift, taper, residual_hbm, dirty_hbm, dirty, sem
):
    slots, columns = collected.shape[:2]
    strip = taper.shape[1]
    groups = strip // LANES // GROUP
    residual_copy = pltpu.make_async_copy(residual, residual_hbm, sem.at[groups])
    residual_copy.start()
    pieces = collected[...].reshape(slots * columns, 2 * XC)
    copies = []
    for group in range(groups):
        for block in range(group * GROUP, (group + 1) * GROUP):
            rows = slice(block * LANES, (block + 1) * LANES)
            back_rows = jnp.dot(pieces, table[block], preferred_element_type=F32)
            real, imag = shift[0, :, rows], shift[1, :, rows]
            strip_sum = jnp.zeros((columns, LANES), F32)
            for i in range(slots):
                own = back_rows[i * columns : (i + 1) * columns]
                strip_sum = strip_sum + real[i : i + 1] * own[:, :LANES]
                strip_sum = strip_sum + imag[i : i + 1] * own[:, LANES:]
            dirty[:, rows] = strip_sum * taper[:, rows]
        rows = pl.ds(group * GROUP * LANES, GROUP * LANES)
        copies.append(pltpu.make_async_copy(dirty.at[:, rows], dirty_hbm.at[:, rows], sem.at[group]))
        copies[-1].start()
    for copy in copies:
        copy.wait()
    residual_copy.wait()


def pin(operand):
    return pltpu.with_memory_space_constraint(operand, pltpu.HBM)


def local(
    sky_image, subgrid_offsets, owner_order, visibility_count, visibility_cell, observed,
    visibility_weight, row_kernel, column_kernel,
):
    facets, bands = lax.axis_size("facet"), lax.axis_size("uv")
    columns, strip = sky_image.shape
    slots = facets
    live_slots = visibility_cell.shape[1]
    vmem = pl.BlockSpec(memory_space=pltpu.VMEM)
    hbm = pl.BlockSpec(memory_space=pltpu.HBM)
    dma = pltpu.SemaphoreType.DMA
    traded = pltpu.VMEM((facets, columns, 2 * XC), BF16)
    kept = pl.pallas_call(
        functools.partial(kernel, facets, bands),
        out_shape=(
            pltpu.VMEM(observed.shape, F32),
            pltpu.VMEM((facets, columns, 2 * XC), BF16),
            pltpu.VMEM((strip // LANES, 2 * XC, 2 * LANES), BF16),
            pltpu.VMEM((2, slots, strip), F32),
            pltpu.VMEM((1, strip), F32),
        ),
        in_specs=[hbm] * 9,
        out_specs=(vmem,) * 5,
        scratch_shapes=[
            pltpu.SMEM(subgrid_offsets.shape, jnp.int32),
            pltpu.SMEM(owner_order.shape, jnp.int32),
            pltpu.SMEM(visibility_count.shape, jnp.int32),
            pltpu.SMEM(row_kernel.shape, F32),
            pltpu.SMEM(column_kernel.shape, F32),
            pltpu.VMEM(visibility_cell.shape, jnp.int32),
            pltpu.VMEM((columns, strip), BF16),
            pltpu.VMEM((2, columns, live_slots), BF16),
            pltpu.VMEM((columns, live_slots), F32),
            pltpu.VMEM((2, 2, 2 * EDGE, live_slots), BF16),
            pltpu.VMEM((2, EDGE, live_slots), F32),
            pltpu.VMEM((columns, strip), F32),
            pltpu.VMEM((slots * columns, 2 * XC), F32),
            traded,
            traded,
            pltpu.VMEM((2 * SG, 2 * live_slots), BF16),
            pltpu.VMEM((columns, 2 * SG), F32),
            pltpu.VMEM((2, EDGE, 2 * SG), F32),
            traded,
            traded,
            dma((10,)),
            dma((facets,)),
            dma((facets,)),
            dma((facets,)),
            dma((facets,)),
            dma((6,)),
            dma((6,)),
        ],
        compiler_params=pltpu.CompilerParams(
            collective_id=0, has_side_effects=True, vmem_limit_bytes=32 * 1024 * 1024
        ),
    )(
        pin(subgrid_offsets), pin(owner_order), visibility_count, pin(row_kernel),
        pin(column_kernel), pin(visibility_cell), pin(sky_image), pin(observed),
        pin(visibility_weight),
    )
    return pl.pallas_call(
        image_kernel,
        out_shape=(
            jax.ShapeDtypeStruct(observed.shape, F32),
            jax.ShapeDtypeStruct(sky_image.shape, F32),
        ),
        in_specs=[vmem] * 5,
        out_specs=(hbm, hbm),
        scratch_shapes=[
            pltpu.VMEM((columns, strip), F32),
            dma((strip // LANES // GROUP + 1,)),
        ],
        compiler_params=pltpu.CompilerParams(vmem_limit_bytes=32 * 1024 * 1024),
    )(*kept)


def solution(mesh):
    in_specs = (
        P("uv", "facet"), P(), P(), P("facet"), P("facet", None), P("facet", None, "uv", None),
        P("facet", "uv", None), P(), P(),
    )
    out_specs = (P("facet", None, "uv", None), P("uv", "facet"))
    return jax.shard_map(local, mesh=mesh, in_specs=in_specs, out_specs=out_specs, check_vma=False)
```

```python
import functools
import math

import jax
import jax.numpy as jnp
from jax import lax
from jax.experimental import pallas as pl
from jax.experimental.pallas import tpu as pltpu
from jax.sharding import PartitionSpec as P

XC = 128
SG = 256
LANES = 128
EDGE = 8
GROUP = 4
F32 = jnp.float32
BF16 = jnp.bfloat16


def sine(a):
    square = a * a
    total = jnp.full_like(a, 1.0 / math.factorial(17))
    for order in range(15, 0, -2):
        sign = -1.0 if order % 4 == 3 else 1.0
        total = total * square + sign / math.factorial(order)
    return a * total


def cosine(a):
    square = a * a
    total = jnp.full_like(a, -1.0 / math.factorial(18))
    for order in range(16, -1, -2):
        sign = -1.0 if order % 4 == 2 else 1.0
        total = total * square + sign / math.factorial(order)
    return total


def turn(steps, period):
    steps = jnp.bitwise_and(steps, period - 1)
    steps = jnp.where(steps >= period // 2, steps - period, steps)
    angle = steps.astype(F32) * (2.0 * math.pi / period)
    return cosine(angle), sine(angle)


def iota(shape, dim):
    return lax.broadcasted_iota(jnp.int32, shape, dim)


def kernel(
    facets, bands, offsets_hbm, owner_hbm, count_hbm, rowk_hbm, colk_hbm, cell_hbm,
    sky_hbm, obs_hbm, wt_hbm,
    residual, collected, table, shift, taper,
    offsets, owner, count, rowk, colk, cell, sky, obs, wt, obs_halo, wt_halo, windowed, across,
    send1, recv1, grid, back_table, z, z_halo, send2, recv2,
    local_sem, send_sem1, recv_sem1, send_sem2, recv_sem2, halo_send, halo_recv,
):
    me = lax.axis_index("facet")
    band = lax.axis_index("uv")
    right, left = lax.rem(band + 1, bands), lax.rem(band + bands - 1, bands)
    columns, strip = sky.shape
    slots = facets
    blocks = strip // LANES
    taps = colk.shape[0]
    margin = (taps - 1) // 2
    live_slots = cell.shape[1]

    sky_copy = pltpu.make_async_copy(sky_hbm, sky, local_sem.at[0])
    obs_copy = pltpu.make_async_copy(obs_hbm.at[0], obs, local_sem.at[1])
    wt_copy = pltpu.make_async_copy(wt_hbm.at[0], wt, local_sem.at[2])
    small = [
        pltpu.make_async_copy(source, target, local_sem.at[4 + i])
        for i, (source, target) in enumerate(
            [
                (offsets_hbm, offsets), (owner_hbm, owner), (count_hbm, count),
                (rowk_hbm, rowk), (colk_hbm, colk), (cell_hbm, cell),
            ]
        )
    ]
    sky_copy.start()
    for copy in small:
        copy.start()
    obs_copy.start()
    wt_copy.start()

    barrier = pltpu.get_barrier_semaphore()

    def greet(d, carry):
        pl.semaphore_signal(
            barrier, inc=1, device_id={"facet": lax.rem(me + d, facets)},
            device_id_type=pl.DeviceIdType.MESH,
        )
        return carry

    lax.fori_loop(1, facets, greet, 0)
    for side in (left, right):
        pl.semaphore_signal(
            barrier, inc=1, device_id={"uv": side}, device_id_type=pl.DeviceIdType.MESH
        )

    def exchange(index, src, dst, side):
        return pltpu.make_async_remote_copy(
            src_ref=src, dst_ref=dst, send_sem=halo_send.at[index],
            recv_sem=halo_recv.at[index], device_id={"uv": side},
            device_id_type=pl.DeviceIdType.MESH,
        )

    half = facets // 2
    high, low = me // half, lax.rem(me, half)

    def peer(d):
        return lax.rem(high + d // half, 2) * half + lax.rem(low + d % half, half)

    def opposite(d):
        return d // half * half + (half - d % half) % half

    def send_contribution(d):
        return pltpu.make_async_remote_copy(
            src_ref=send1.at[d], dst_ref=recv1.at[me], send_sem=send_sem1.at[d],
            recv_sem=recv_sem1.at[opposite(d)], device_id={"facet": peer(d)},
            device_id_type=pl.DeviceIdType.MESH,
        )

    def take_contribution(d):
        return pltpu.make_async_remote_copy(
            src_ref=send1.at[d], dst_ref=recv1.at[peer(d)], send_sem=send_sem1.at[d],
            recv_sem=recv_sem1.at[d], device_id={"facet": peer(d)},
            device_id_type=pl.DeviceIdType.MESH,
        )

    def send_pieces(d):
        return pltpu.make_async_remote_copy(
            src_ref=send2.at[peer(d)], dst_ref=recv2.at[opposite(d)], send_sem=send_sem2.at[d],
            recv_sem=recv_sem2.at[opposite(d)], device_id={"facet": peer(d)},
            device_id_type=pl.DeviceIdType.MESH,
        )

    def take_pieces(d):
        return pltpu.make_async_remote_copy(
            src_ref=send2.at[peer(d)], dst_ref=recv2.at[d], send_sem=send_sem2.at[d],
            recv_sem=recv_sem2.at[d], device_id={"facet": peer(d)},
            device_id_type=pl.DeviceIdType.MESH,
        )

    order = list(range(half, facets)) + list(range(1, half))

    position = iota((1, strip), 1)
    taper[...] = sine((position.astype(F32) + 0.5) * (math.pi / strip)) * (1.0 / math.sqrt(strip))
    frequency = iota((LANES, XC), 1)
    first = (2 * me + 1) * (strip // facets)
    start = turn(frequency * (iota((LANES, XC), 0) + first), strip)
    step_cos, step_sin = turn(frequency * LANES, strip)
    for copy in small:
        copy.wait()
    offset = jnp.zeros((slots, strip), jnp.int32)
    slot_row = iota((slots, strip), 0)
    for i in range(slots):
        offset = jnp.where(slot_row == i, offsets[owner[peer(i)]], offset)
    shift_cos, shift_sin = turn(offset * iota((slots, strip), 1), strip)
    shift[0] = shift_cos
    shift[1] = -shift_sin
    sky_copy.wait()
    windowed[...] = (sky[...].astype(F32) * taper[...]).astype(BF16).astype(F32)
    def contribute(lowest, make_table):
        c, s = start
        total = jnp.zeros((half * columns, 2 * XC), F32)
        for group in range(blocks // GROUP):
            pieces = []
            for block in range(group * GROUP, (group + 1) * GROUP):
                if make_table:
                    left_part = jnp.concatenate([c, s], axis=0)
                    right_part = jnp.concatenate([-s, c], axis=0)
                    across[pl.ds(block * 2 * LANES, 2 * LANES)] = jnp.concatenate(
                        [left_part, right_part], axis=1
                    ).astype(BF16)
                    c, s = c * step_cos - s * step_sin, s * step_cos + c * step_sin
                rows = slice(block * LANES, (block + 1) * LANES)
                piece = windowed[:, rows]
                real, imag = shift[0, :, rows], shift[1, :, rows]
                pieces.append(
                    jnp.concatenate(
                        [
                            jnp.concatenate(
                                [real[i : i + 1] * piece, imag[i : i + 1] * piece], axis=1
                            ).astype(BF16)
                            for i in range(lowest, lowest + half)
                        ],
                        axis=0,
                    )
                )
            depth = GROUP * 2 * LANES
            total = total + jnp.dot(
                jnp.concatenate(pieces, axis=1), across[pl.ds(group * depth, depth)],
                preferred_element_type=F32,
            )
        send1[lowest : lowest + half] = total.astype(BF16).reshape(half, columns, 2 * XC)

    contribute(half, True)
    pl.semaphore_wait(barrier, facets + 1)
    for d in range(half, facets):
        send_contribution(d).start()
    contribute(0, False)
    for d in range(1, half):
        send_contribution(d).start()
    recv1[me] = send1[0]
    early = [
        exchange(0, obs_hbm.at[0, :, pl.ds(columns - 2 * EDGE, 2 * EDGE)], obs_halo.at[0], right),
        exchange(1, obs_hbm.at[0, :, pl.ds(0, 2 * EDGE)], obs_halo.at[1], left),
        exchange(2, wt_hbm.at[0, pl.ds(columns - EDGE, EDGE)], wt_halo.at[0], right),
        exchange(3, wt_hbm.at[0, pl.ds(0, EDGE)], wt_halo.at[1], left),
    ]
    for copy in early:
        copy.start()

    factor = 1.0 / math.sqrt(facets * XC)
    fine_cos, fine_sin = turn(iota((SG, SG), 0) * iota((SG, SG), 1), SG)
    fine_cos = (fine_cos * factor).astype(BF16)
    fine_sin = (fine_sin * factor).astype(BF16)
    distance = iota((SG, live_slots), 0) - cell[...] + margin
    degrid = jnp.zeros((SG, live_slots), F32)
    for t in range(taps):
        degrid = jnp.where(distance == t, rowk[t], degrid)
    degrid_back = jnp.transpose(degrid).astype(BF16)
    degrid = degrid.astype(BF16)
    grid_cos = jnp.dot(fine_cos, degrid, preferred_element_type=F32)
    grid_sin = jnp.dot(fine_sin, degrid, preferred_element_type=F32)
    grid[0:SG, 0:live_slots] = grid_cos.astype(BF16)
    grid[0:SG, live_slots:] = grid_sin.astype(BF16)
    grid[SG:, 0:live_slots] = (-grid_sin).astype(BF16)
    grid[SG:, live_slots:] = grid_cos.astype(BF16)

    grid_cos = jnp.dot(degrid_back, fine_cos, preferred_element_type=F32)
    grid_sin = jnp.dot(degrid_back, fine_sin, preferred_element_type=F32)
    back_table[0:live_slots, 0:SG] = grid_cos.astype(BF16)
    back_table[0:live_slots, SG:] = (-grid_sin).astype(BF16)
    back_table[live_slots:, 0:SG] = grid_sin.astype(BF16)
    back_table[live_slots:, SG:] = grid_cos.astype(BF16)

    c, s = jnp.transpose(start[0]), jnp.transpose(start[1])
    turn_cos, turn_sin = jnp.transpose(step_cos), jnp.transpose(step_sin)
    for block in range(blocks):
        upper = jnp.concatenate([c, s], axis=1)
        lower = jnp.concatenate([-s, c], axis=1)
        table[block] = jnp.concatenate([upper, lower], axis=0).astype(BF16)
        c, s = c * turn_cos - s * turn_sin, s * turn_cos + c * turn_sin

    for d in order:
        take_contribution(d).wait_recv()
    blank = jnp.zeros((columns, SG - XC), F32)
    sums = [jnp.zeros((columns, SG), F32), jnp.zeros((columns, SG), F32)]
    for f in range(facets):
        place = (2 * f + 1) * (SG // (2 * facets)) % SG
        arrived = recv1[f].astype(F32)
        for q in range(2):
            wide = jnp.concatenate([arrived[:, q * XC : (q + 1) * XC], blank], axis=1)
            sums[q] = sums[q] + pltpu.roll(wide, place, 1)
    z[...] = jnp.concatenate(sums, axis=1)
    late = [
        exchange(4, z.at[pl.ds(columns - EDGE, EDGE)], z_halo.at[0], right),
        exchange(5, z.at[pl.ds(0, EDGE)], z_halo.at[1], left),
    ]
    for copy in late:
        copy.start()

    obs_copy.wait()
    wt_copy.wait()
    for copy in early:
        copy.wait_recv()
    for copy in late:
        copy.wait_recv()
    rows = columns + 2 * EDGE
    before = jnp.where(band == 0, 0.0, z_halo[0])
    after = jnp.where(band == bands - 1, 0.0, z_halo[1])
    padded = jnp.concatenate([before, z[...], after], axis=0)
    convolved = jnp.zeros_like(padded)
    for t in range(taps):
        convolved = convolved + colk[t] * pltpu.roll(padded, (margin - t) % rows, 0)
    model = jnp.dot(convolved.astype(BF16), grid[...], preferred_element_type=F32)
    row = iota((rows, live_slots), 0)
    lowest = jnp.where(band == 0, EDGE, EDGE - margin)
    highest = jnp.where(band == bands - 1, EDGE + columns, EDGE + columns + margin)
    valid = (row >= lowest) & (row < highest) & (iota((rows, live_slots), 1) < count[0])
    weight = jnp.where(valid, jnp.concatenate([wt_halo[0], wt[...], wt_halo[1]], axis=0), 0.0)
    parts = []
    for p in range(2):
        seen = jnp.concatenate(
            [
                obs_halo[0, p].astype(F32)[EDGE:],
                obs[p].astype(F32),
                obs_halo[1, p].astype(F32)[:EDGE],
            ],
            axis=0,
        )
        parts.append(weight * (seen - model[:, p * live_slots : (p + 1) * live_slots]))
        residual[0, p] = parts[p][EDGE : EDGE + columns]
    rounded = jnp.concatenate(parts, axis=1).astype(BF16)
    gridded = jnp.dot(rounded, back_table[...], preferred_element_type=F32)
    back = jnp.zeros_like(gridded)
    for t in range(taps):
        back = back + colk[t] * pltpu.roll(gridded, (t - margin) % rows, 0)
    back = back[EDGE : EDGE + columns]
    for f in range(facets):
        place = (2 * f + 1) * (SG // (2 * facets)) % SG
        send2[f] = jnp.concatenate(
            [
                pltpu.roll(back[:, p * SG : (p + 1) * SG], (SG - place) % SG, 1)[:, :XC]
                for p in range(2)
            ],
            axis=1,
        ).astype(BF16)
    for d in order:
        send_pieces(d).start()
    recv2[0] = send2[me]
    for copy in early + late:
        copy.wait_send()
    for d in order:
        send_contribution(d).wait_send()
    for d in order:
        take_pieces(d).wait_recv()
    collected[...] = recv2[...]
    for d in order:
        send_pieces(d).wait_send()


def image_kernel(
    residual, collected, table, shift, taper, residual_hbm, dirty_hbm, dirty, sem
):
    slots, columns = collected.shape[:2]
    strip = taper.shape[1]
    groups = strip // LANES // GROUP
    residual_copy = pltpu.make_async_copy(residual, residual_hbm, sem.at[groups])
    residual_copy.start()
    pieces = collected[...].reshape(slots * columns, 2 * XC)
    copies = []
    for group in range(groups):
        for block in range(group * GROUP, (group + 1) * GROUP):
            rows = slice(block * LANES, (block + 1) * LANES)
            back_rows = jnp.dot(pieces, table[block], preferred_element_type=F32)
            real, imag = shift[0, :, rows], shift[1, :, rows]
            strip_sum = jnp.zeros((columns, LANES), F32)
            for i in range(slots):
                own = back_rows[i * columns : (i + 1) * columns]
                strip_sum = strip_sum + real[i : i + 1] * own[:, :LANES]
                strip_sum = strip_sum + imag[i : i + 1] * own[:, LANES:]
            dirty[:, rows] = strip_sum * taper[:, rows]
        rows = pl.ds(group * GROUP * LANES, GROUP * LANES)
        copies.append(pltpu.make_async_copy(dirty.at[:, rows], dirty_hbm.at[:, rows], sem.at[group]))
        copies[-1].start()
    for copy in copies:
        copy.wait()
    residual_copy.wait()


def pin(operand):
    return pltpu.with_memory_space_constraint(operand, pltpu.HBM)


def local(
    sky_image, subgrid_offsets, owner_order, visibility_count, visibility_cell, observed,
    visibility_weight, row_kernel, column_kernel,
):
    facets, bands = lax.axis_size("facet"), lax.axis_size("uv")
    columns, strip = sky_image.shape
    slots = facets
    live_slots = visibility_cell.shape[1]
    vmem = pl.BlockSpec(memory_space=pltpu.VMEM)
    hbm = pl.BlockSpec(memory_space=pltpu.HBM)
    dma = pltpu.SemaphoreType.DMA
    traded = pltpu.VMEM((facets, columns, 2 * XC), BF16)
    kept = pl.pallas_call(
        functools.partial(kernel, facets, bands),
        out_shape=(
            pltpu.VMEM(observed.shape, F32),
            pltpu.VMEM((facets, columns, 2 * XC), BF16),
            pltpu.VMEM((strip // LANES, 2 * XC, 2 * LANES), BF16),
            pltpu.VMEM((2, slots, strip), F32),
            pltpu.VMEM((1, strip), F32),
        ),
        in_specs=[hbm] * 9,
        out_specs=(vmem,) * 5,
        scratch_shapes=[
            pltpu.SMEM(subgrid_offsets.shape, jnp.int32),
            pltpu.SMEM(owner_order.shape, jnp.int32),
            pltpu.SMEM(visibility_count.shape, jnp.int32),
            pltpu.SMEM(row_kernel.shape, F32),
            pltpu.SMEM(column_kernel.shape, F32),
            pltpu.VMEM(visibility_cell.shape, jnp.int32),
            pltpu.VMEM((columns, strip), BF16),
            pltpu.VMEM((2, columns, live_slots), BF16),
            pltpu.VMEM((columns, live_slots), F32),
            pltpu.VMEM((2, 2, 2 * EDGE, live_slots), BF16),
            pltpu.VMEM((2, EDGE, live_slots), F32),
            pltpu.VMEM((columns, strip), F32),
            pltpu.VMEM((2 * strip, 2 * XC), BF16),
            traded,
            traded,
            pltpu.VMEM((2 * SG, 2 * live_slots), BF16),
            pltpu.VMEM((2 * live_slots, 2 * SG), BF16),
            pltpu.VMEM((columns, 2 * SG), F32),
            pltpu.VMEM((2, EDGE, 2 * SG), F32),
            traded,
            traded,
            dma((10,)),
            dma((facets,)),
            dma((facets,)),
            dma((facets,)),
            dma((facets,)),
            dma((6,)),
            dma((6,)),
        ],
        compiler_params=pltpu.CompilerParams(
            collective_id=0, has_side_effects=True, vmem_limit_bytes=32 * 1024 * 1024
        ),
    )(
        pin(subgrid_offsets), pin(owner_order), visibility_count, pin(row_kernel),
        pin(column_kernel), pin(visibility_cell), pin(sky_image), pin(observed),
        pin(visibility_weight),
    )
    return pl.pallas_call(
        image_kernel,
        out_shape=(
            jax.ShapeDtypeStruct(observed.shape, F32),
            jax.ShapeDtypeStruct(sky_image.shape, F32),
        ),
        in_specs=[vmem] * 5,
        out_specs=(hbm, hbm),
        scratch_shapes=[
            pltpu.VMEM((columns, strip), F32),
            dma((strip // LANES // GROUP + 1,)),
        ],
        compiler_params=pltpu.CompilerParams(vmem_limit_bytes=32 * 1024 * 1024),
    )(*kept)


def solution(mesh):
    in_specs = (
        P("uv", "facet"), P(), P(), P("facet"), P("facet", None), P("facet", None, "uv", None),
        P("facet", "uv", None), P(), P(),
    )
    out_specs = (P("facet", None, "uv", None), P("uv", "facet"))
    return jax.shard_map(local, mesh=mesh, in_specs=in_specs, out_specs=out_specs, check_vma=False)
```

```python
import functools
import math

import jax
import jax.numpy as jnp
from jax import lax
from jax.experimental import pallas as pl
from jax.experimental.pallas import tpu as pltpu
from jax.sharding import PartitionSpec as P

XC = 128
SG = 256
LANES = 128
EDGE = 8
GROUP = 4
STEP = 16
F32 = jnp.float32
BF16 = jnp.bfloat16


def sine(a):
    square = a * a
    total = jnp.full_like(a, 1.0 / math.factorial(17))
    for order in range(15, 0, -2):
        sign = -1.0 if order % 4 == 3 else 1.0
        total = total * square + sign / math.factorial(order)
    return a * total


def cosine(a):
    square = a * a
    total = jnp.full_like(a, -1.0 / math.factorial(18))
    for order in range(16, -1, -2):
        sign = -1.0 if order % 4 == 2 else 1.0
        total = total * square + sign / math.factorial(order)
    return total


def turn(steps, period):
    steps = jnp.bitwise_and(steps, period - 1)
    steps = jnp.where(steps >= period // 2, steps - period, steps)
    angle = steps.astype(F32) * (2.0 * math.pi / period)
    return cosine(angle), sine(angle)


def iota(shape, dim):
    return lax.broadcasted_iota(jnp.int32, shape, dim)


def kernel(
    facets, bands, offsets_hbm, owner_hbm, count_hbm, rowk_hbm, colk_hbm, cell_hbm,
    sky_hbm, obs_hbm, wt_hbm,
    residual, collected, table, shift, taper,
    offsets, owner, count, rowk, colk, cell, sky, obs, wt, obs_halo, wt_halo, windowed, across,
    send1, recv1, grid, back_table, z, z_halo, send2, recv2,
    local_sem, send_sem1, recv_sem1, send_sem2, recv_sem2, halo_send, halo_recv,
):
    me = lax.axis_index("facet")
    band = lax.axis_index("uv")
    right, left = lax.rem(band + 1, bands), lax.rem(band + bands - 1, bands)
    columns, strip = sky.shape
    slots = facets
    blocks = strip // LANES
    taps = colk.shape[0]
    margin = (taps - 1) // 2
    live_slots = cell.shape[1]

    sky_copy = pltpu.make_async_copy(sky_hbm, sky, local_sem.at[0])
    obs_copy = pltpu.make_async_copy(obs_hbm.at[0], obs, local_sem.at[1])
    wt_copy = pltpu.make_async_copy(wt_hbm.at[0], wt, local_sem.at[2])
    small = [
        pltpu.make_async_copy(source, target, local_sem.at[4 + i])
        for i, (source, target) in enumerate(
            [
                (offsets_hbm, offsets), (owner_hbm, owner), (count_hbm, count),
                (rowk_hbm, rowk), (colk_hbm, colk), (cell_hbm, cell),
            ]
        )
    ]
    sky_copy.start()
    for copy in small:
        copy.start()
    obs_copy.start()
    wt_copy.start()

    barrier = pltpu.get_barrier_semaphore()

    def greet(d, carry):
        pl.semaphore_signal(
            barrier, inc=1, device_id={"facet": lax.rem(me + d, facets)},
            device_id_type=pl.DeviceIdType.MESH,
        )
        return carry

    lax.fori_loop(1, facets, greet, 0)
    for side in (left, right):
        pl.semaphore_signal(
            barrier, inc=1, device_id={"uv": side}, device_id_type=pl.DeviceIdType.MESH
        )

    def exchange(index, src, dst, side):
        return pltpu.make_async_remote_copy(
            src_ref=src, dst_ref=dst, send_sem=halo_send.at[index],
            recv_sem=halo_recv.at[index], device_id={"uv": side},
            device_id_type=pl.DeviceIdType.MESH,
        )

    half = facets // 2
    high, low = me // half, lax.rem(me, half)

    def peer(d):
        return lax.rem(high + d // half, 2) * half + lax.rem(low + d % half, half)

    def opposite(d):
        return d // half * half + (half - d % half) % half

    def send_contribution(d):
        return pltpu.make_async_remote_copy(
            src_ref=send1.at[d], dst_ref=recv1.at[me], send_sem=send_sem1.at[d],
            recv_sem=recv_sem1.at[opposite(d)], device_id={"facet": peer(d)},
            device_id_type=pl.DeviceIdType.MESH,
        )

    def take_contribution(d):
        return pltpu.make_async_remote_copy(
            src_ref=send1.at[d], dst_ref=recv1.at[peer(d)], send_sem=send_sem1.at[d],
            recv_sem=recv_sem1.at[d], device_id={"facet": peer(d)},
            device_id_type=pl.DeviceIdType.MESH,
        )

    def send_pieces(d):
        return pltpu.make_async_remote_copy(
            src_ref=send2.at[peer(d)], dst_ref=recv2.at[opposite(d)], send_sem=send_sem2.at[d],
            recv_sem=recv_sem2.at[opposite(d)], device_id={"facet": peer(d)},
            device_id_type=pl.DeviceIdType.MESH,
        )

    def take_pieces(d):
        return pltpu.make_async_remote_copy(
            src_ref=send2.at[peer(d)], dst_ref=recv2.at[d], send_sem=send_sem2.at[d],
            recv_sem=recv_sem2.at[d], device_id={"facet": peer(d)},
            device_id_type=pl.DeviceIdType.MESH,
        )

    order = list(range(half, facets)) + list(range(1, half))

    position = iota((1, strip), 1)
    taper[...] = sine((position.astype(F32) + 0.5) * (math.pi / strip)) * (1.0 / math.sqrt(strip))
    frequency = iota((LANES, XC), 1)
    first = (2 * me + 1) * (strip // facets)
    start = turn(frequency * (iota((LANES, XC), 0) + first), strip)
    step_cos, step_sin = turn(frequency[0:1] * LANES, strip)
    for copy in small:
        copy.wait()
    offset = jnp.zeros((slots, LANES), jnp.int32)
    slot_row = iota((slots, LANES), 0)
    for i in range(slots):
        offset = jnp.where(slot_row == i, offsets[owner[peer(i)]], offset)
    c, s = turn(offset * iota((slots, LANES), 1), strip)
    ahead_cos, ahead_sin = turn(offset * LANES, strip)
    for block in range(blocks):
        rows = slice(block * LANES, (block + 1) * LANES)
        shift[0, :, rows] = c
        shift[1, :, rows] = -s
        c, s = c * ahead_cos - s * ahead_sin, s * ahead_cos + c * ahead_sin
    sky_copy.wait()
    windowed[...] = (sky[...].astype(F32) * taper[...]).astype(BF16).astype(F32)
    def contribute(lowest, make_table):
        c, s = start
        total = jnp.zeros((half * columns, 2 * XC), F32)
        for group in range(blocks // GROUP):
            pieces = []
            for block in range(group * GROUP, (group + 1) * GROUP):
                if make_table:
                    left_part = jnp.concatenate([c, s], axis=0)
                    right_part = jnp.concatenate([-s, c], axis=0)
                    across[pl.ds(block * 2 * LANES, 2 * LANES)] = jnp.concatenate(
                        [left_part, right_part], axis=1
                    ).astype(BF16)
                    c, s = c * step_cos - s * step_sin, s * step_cos + c * step_sin
                rows = slice(block * LANES, (block + 1) * LANES)
                piece = windowed[:, rows]
                real, imag = shift[0, :, rows], shift[1, :, rows]
                pieces.append(
                    jnp.concatenate(
                        [
                            jnp.concatenate(
                                [real[i : i + 1] * piece, imag[i : i + 1] * piece], axis=1
                            ).astype(BF16)
                            for i in range(lowest, lowest + half)
                        ],
                        axis=0,
                    )
                )
            depth = GROUP * 2 * LANES
            total = total + jnp.dot(
                jnp.concatenate(pieces, axis=1), across[pl.ds(group * depth, depth)],
                preferred_element_type=F32,
            )
        send1[lowest : lowest + half] = total.astype(BF16).reshape(half, columns, 2 * XC)

    contribute(half, True)
    pl.semaphore_wait(barrier, facets + 1)
    for d in range(half, facets):
        send_contribution(d).start()
    contribute(0, False)
    for d in range(1, half):
        send_contribution(d).start()
    recv1[me] = send1[0]
    early = [
        exchange(0, obs_hbm.at[0, :, pl.ds(columns - 2 * EDGE, 2 * EDGE)], obs_halo.at[0], right),
        exchange(1, obs_hbm.at[0, :, pl.ds(0, 2 * EDGE)], obs_halo.at[1], left),
        exchange(2, wt_hbm.at[0, pl.ds(columns - EDGE, EDGE)], wt_halo.at[0], right),
        exchange(3, wt_hbm.at[0, pl.ds(0, EDGE)], wt_halo.at[1], left),
    ]
    for copy in early:
        copy.start()

    factor = 1.0 / math.sqrt(facets * XC)
    c, s = turn(iota((STEP, SG), 0) * iota((STEP, SG), 1), SG)
    c, s = c * factor, s * factor
    ahead_cos, ahead_sin = turn(iota((1, SG), 1) * STEP, SG)
    cosines, sines = [], []
    for _ in range(SG // STEP):
        cosines.append(c.astype(BF16))
        sines.append(s.astype(BF16))
        c, s = c * ahead_cos - s * ahead_sin, s * ahead_cos + c * ahead_sin
    fine_cos, fine_sin = jnp.concatenate(cosines, axis=0), jnp.concatenate(sines, axis=0)
    distance = iota((SG, live_slots), 0) - cell[...] + margin
    degrid = jnp.zeros((SG, live_slots), F32)
    for t in range(taps):
        degrid = jnp.where(distance == t, rowk[t], degrid)
    degrid = degrid.astype(BF16)
    grid_cos = jnp.dot(fine_cos, degrid, preferred_element_type=F32)
    grid_sin = jnp.dot(fine_sin, degrid, preferred_element_type=F32)
    grid[0:SG, 0:live_slots] = grid_cos.astype(BF16)
    grid[0:SG, live_slots:] = grid_sin.astype(BF16)
    grid[SG:, 0:live_slots] = (-grid_sin).astype(BF16)
    grid[SG:, live_slots:] = grid_cos.astype(BF16)

    for d in order:
        take_contribution(d).wait_recv()
    blank = jnp.zeros((columns, SG - XC), F32)
    sums = [jnp.zeros((columns, SG), F32), jnp.zeros((columns, SG), F32)]
    for f in range(facets):
        place = (2 * f + 1) * (SG // (2 * facets)) % SG
        arrived = recv1[f].astype(F32)
        for q in range(2):
            wide = jnp.concatenate([arrived[:, q * XC : (q + 1) * XC], blank], axis=1)
            sums[q] = sums[q] + pltpu.roll(wide, place, 1)
    z[...] = jnp.concatenate(sums, axis=1)
    late = [
        exchange(4, z.at[pl.ds(columns - EDGE, EDGE)], z_halo.at[0], right),
        exchange(5, z.at[pl.ds(0, EDGE)], z_halo.at[1], left),
    ]
    for copy in late:
        copy.start()

    degrid_back = jnp.transpose(degrid.astype(F32)).astype(BF16)
    grid_cos = jnp.dot(degrid_back, fine_cos, preferred_element_type=F32)
    grid_sin = jnp.dot(degrid_back, fine_sin, preferred_element_type=F32)
    back_table[0:live_slots, 0:SG] = grid_cos.astype(BF16)
    back_table[0:live_slots, SG:] = (-grid_sin).astype(BF16)
    back_table[live_slots:, 0:SG] = grid_sin.astype(BF16)
    back_table[live_slots:, SG:] = grid_cos.astype(BF16)


    obs_copy.wait()
    wt_copy.wait()
    for copy in early:
        copy.wait_recv()
    for copy in late:
        copy.wait_recv()
    rows = columns + 2 * EDGE
    before = jnp.where(band == 0, 0.0, z_halo[0])
    after = jnp.where(band == bands - 1, 0.0, z_halo[1])
    padded = jnp.concatenate([before, z[...], after], axis=0)
    convolved = jnp.zeros_like(padded)
    for t in range(taps):
        convolved = convolved + colk[t] * pltpu.roll(padded, (margin - t) % rows, 0)
    model = jnp.dot(convolved.astype(BF16), grid[...], preferred_element_type=F32)
    row = iota((rows, live_slots), 0)
    lowest = jnp.where(band == 0, EDGE, EDGE - margin)
    highest = jnp.where(band == bands - 1, EDGE + columns, EDGE + columns + margin)
    valid = (row >= lowest) & (row < highest) & (iota((rows, live_slots), 1) < count[0])
    weight = jnp.where(valid, jnp.concatenate([wt_halo[0], wt[...], wt_halo[1]], axis=0), 0.0)
    parts = []
    for p in range(2):
        seen = jnp.concatenate(
            [
                obs_halo[0, p].astype(F32)[EDGE:],
                obs[p].astype(F32),
                obs_halo[1, p].astype(F32)[:EDGE],
            ],
            axis=0,
        )
        parts.append(weight * (seen - model[:, p * live_slots : (p + 1) * live_slots]))
        residual[0, p] = parts[p][EDGE : EDGE + columns]
    rounded = jnp.concatenate(parts, axis=1).astype(BF16)
    gridded = jnp.dot(rounded, back_table[...], preferred_element_type=F32)
    back = jnp.zeros_like(gridded)
    for t in range(taps):
        back = back + colk[t] * pltpu.roll(gridded, (t - margin) % rows, 0)
    back = back[EDGE : EDGE + columns]
    for f in range(facets):
        place = (2 * f + 1) * (SG // (2 * facets)) % SG
        send2[f] = jnp.concatenate(
            [
                pltpu.roll(back[:, p * SG : (p + 1) * SG], (SG - place) % SG, 1)[:, :XC]
                for p in range(2)
            ],
            axis=1,
        ).astype(BF16)
    for d in order:
        send_pieces(d).start()
    recv2[0] = send2[me]

    c, s = jnp.transpose(start[0]), jnp.transpose(start[1])
    turn_cos = jnp.transpose(jnp.broadcast_to(step_cos, (LANES, XC)))
    turn_sin = jnp.transpose(jnp.broadcast_to(step_sin, (LANES, XC)))
    for block in range(blocks):
        upper = jnp.concatenate([c, s], axis=1)
        lower = jnp.concatenate([-s, c], axis=1)
        table[block] = jnp.concatenate([upper, lower], axis=0).astype(BF16)
        c, s = c * turn_cos - s * turn_sin, s * turn_cos + c * turn_sin

    for copy in early + late:
        copy.wait_send()
    for d in order:
        send_contribution(d).wait_send()
    for d in order:
        take_pieces(d).wait_recv()
    collected[...] = recv2[...]
    for d in order:
        send_pieces(d).wait_send()


def image_kernel(
    residual, collected, table, shift, taper, residual_hbm, dirty_hbm, dirty, sem
):
    slots, columns = collected.shape[:2]
    strip = taper.shape[1]
    groups = strip // LANES // GROUP
    residual_copy = pltpu.make_async_copy(residual, residual_hbm, sem.at[groups])
    residual_copy.start()
    pieces = collected[...].reshape(slots * columns, 2 * XC)
    copies = []
    for group in range(groups):
        for block in range(group * GROUP, (group + 1) * GROUP):
            rows = slice(block * LANES, (block + 1) * LANES)
            back_rows = jnp.dot(pieces, table[block], preferred_element_type=F32)
            real, imag = shift[0, :, rows], shift[1, :, rows]
            strip_sum = jnp.zeros((columns, LANES), F32)
            for i in range(slots):
                own = back_rows[i * columns : (i + 1) * columns]
                strip_sum = strip_sum + real[i : i + 1] * own[:, :LANES]
                strip_sum = strip_sum + imag[i : i + 1] * own[:, LANES:]
            dirty[:, rows] = strip_sum * taper[:, rows]
        rows = pl.ds(group * GROUP * LANES, GROUP * LANES)
        copies.append(pltpu.make_async_copy(dirty.at[:, rows], dirty_hbm.at[:, rows], sem.at[group]))
        copies[-1].start()
    for copy in copies:
        copy.wait()
    residual_copy.wait()


def pin(operand):
    return pltpu.with_memory_space_constraint(operand, pltpu.HBM)


def local(
    sky_image, subgrid_offsets, owner_order, visibility_count, visibility_cell, observed,
    visibility_weight, row_kernel, column_kernel,
):
    facets, bands = lax.axis_size("facet"), lax.axis_size("uv")
    columns, strip = sky_image.shape
    slots = facets
    live_slots = visibility_cell.shape[1]
    vmem = pl.BlockSpec(memory_space=pltpu.VMEM)
    hbm = pl.BlockSpec(memory_space=pltpu.HBM)
    dma = pltpu.SemaphoreType.DMA
    traded = pltpu.VMEM((facets, columns, 2 * XC), BF16)
    kept = pl.pallas_call(
        functools.partial(kernel, facets, bands),
        out_shape=(
            pltpu.VMEM(observed.shape, F32),
            pltpu.VMEM((facets, columns, 2 * XC), BF16),
            pltpu.VMEM((strip // LANES, 2 * XC, 2 * LANES), BF16),
            pltpu.VMEM((2, slots, strip), F32),
            pltpu.VMEM((1, strip), F32),
        ),
        in_specs=[hbm] * 9,
        out_specs=(vmem,) * 5,
        scratch_shapes=[
            pltpu.SMEM(subgrid_offsets.shape, jnp.int32),
            pltpu.SMEM(owner_order.shape, jnp.int32),
            pltpu.SMEM(visibility_count.shape, jnp.int32),
            pltpu.SMEM(row_kernel.shape, F32),
            pltpu.SMEM(column_kernel.shape, F32),
            pltpu.VMEM(visibility_cell.shape, jnp.int32),
            pltpu.VMEM((columns, strip), BF16),
            pltpu.VMEM((2, columns, live_slots), BF16),
            pltpu.VMEM((columns, live_slots), F32),
            pltpu.VMEM((2, 2, 2 * EDGE, live_slots), BF16),
            pltpu.VMEM((2, EDGE, live_slots), F32),
            pltpu.VMEM((columns, strip), F32),
            pltpu.VMEM((2 * strip, 2 * XC), BF16),
            traded,
            traded,
            pltpu.VMEM((2 * SG, 2 * live_slots), BF16),
            pltpu.VMEM((2 * live_slots, 2 * SG), BF16),
            pltpu.VMEM((columns, 2 * SG), F32),
            pltpu.VMEM((2, EDGE, 2 * SG), F32),
            traded,
            traded,
            dma((10,)),
            dma((facets,)),
            dma((facets,)),
            dma((facets,)),
            dma((facets,)),
            dma((6,)),
            dma((6,)),
        ],
        compiler_params=pltpu.CompilerParams(
            collective_id=0, has_side_effects=True, vmem_limit_bytes=32 * 1024 * 1024
        ),
    )(
        pin(subgrid_offsets), pin(owner_order), visibility_count, pin(row_kernel),
        pin(column_kernel), pin(visibility_cell), pin(sky_image), pin(observed),
        pin(visibility_weight),
    )
    return pl.pallas_call(
        image_kernel,
        out_shape=(
            jax.ShapeDtypeStruct(observed.shape, F32),
            jax.ShapeDtypeStruct(sky_image.shape, F32),
        ),
        in_specs=[vmem] * 5,
        out_specs=(hbm, hbm),
        scratch_shapes=[
            pltpu.VMEM((columns, strip), F32),
            dma((strip // LANES // GROUP + 1,)),
        ],
        compiler_params=pltpu.CompilerParams(vmem_limit_bytes=32 * 1024 * 1024),
    )(*kept)


def solution(mesh):
    in_specs = (
        P("uv", "facet"), P(), P(), P("facet"), P("facet", None), P("facet", None, "uv", None),
        P("facet", "uv", None), P(), P(),
    )
    out_specs = (P("facet", None, "uv", None), P("uv", "facet"))
    return jax.shard_map(local, mesh=mesh, in_specs=in_specs, out_specs=out_specs, check_vma=False)
```

```python
import functools
import math

import jax
import jax.numpy as jnp
from jax import lax
from jax.experimental import pallas as pl
from jax.experimental.pallas import tpu as pltpu
from jax.sharding import PartitionSpec as P

XC = 128
SG = 256
LANES = 128
EDGE = 8
GROUP = 4
STEP = 16
F32 = jnp.float32
BF16 = jnp.bfloat16


def sine(a):
    square = a * a
    total = jnp.full_like(a, 1.0 / math.factorial(17))
    for order in range(15, 0, -2):
        sign = -1.0 if order % 4 == 3 else 1.0
        total = total * square + sign / math.factorial(order)
    return a * total


def cosine(a):
    square = a * a
    total = jnp.full_like(a, -1.0 / math.factorial(18))
    for order in range(16, -1, -2):
        sign = -1.0 if order % 4 == 2 else 1.0
        total = total * square + sign / math.factorial(order)
    return total


def turn(steps, period):
    steps = jnp.bitwise_and(steps, period - 1)
    steps = jnp.where(steps >= period // 2, steps - period, steps)
    angle = steps.astype(F32) * (2.0 * math.pi / period)
    return cosine(angle), sine(angle)


def iota(shape, dim):
    return lax.broadcasted_iota(jnp.int32, shape, dim)


def image_sum(pieces, lowest, table, shift, target, finish, store):
    slots, columns = pieces.shape[:2]
    pieces = pieces.reshape(slots * columns, pieces.shape[2])
    for block in range(table.shape[0]):
        rows = slice(block * LANES, (block + 1) * LANES)
        back_rows = jnp.dot(pieces, table[block], preferred_element_type=F32)
        real = shift[0, lowest : lowest + slots, rows]
        imag = shift[1, lowest : lowest + slots, rows]
        strip_sum = jnp.zeros((columns, LANES), F32)
        if finish is not None:
            strip_sum = finish[0][:, rows]
        for i in range(slots):
            own = back_rows[i * columns : (i + 1) * columns]
            strip_sum = strip_sum + real[i : i + 1] * own[:, :LANES]
            strip_sum = strip_sum + imag[i : i + 1] * own[:, LANES:]
        if finish is not None:
            strip_sum = strip_sum * finish[1][:, rows]
        target[:, rows] = strip_sum
        if store is not None:
            store(block)


def kernel(
    facets, bands, offsets_hbm, owner_hbm, count_hbm, rowk_hbm, colk_hbm, cell_hbm,
    sky_hbm, obs_hbm, wt_hbm,
    residual, collected, partial, table, shift, taper,
    offsets, owner, count, rowk, colk, cell, sky, obs, wt, obs_halo, wt_halo, windowed, across,
    send1, recv1, grid, back_table, z, z_halo, send2, recv2,
    local_sem, send_sem1, recv_sem1, send_sem2, recv_sem2, halo_send, halo_recv,
):
    me = lax.axis_index("facet")
    band = lax.axis_index("uv")
    right, left = lax.rem(band + 1, bands), lax.rem(band + bands - 1, bands)
    columns, strip = sky.shape
    slots = facets
    blocks = strip // LANES
    taps = colk.shape[0]
    margin = (taps - 1) // 2
    live_slots = cell.shape[1]

    sky_copy = pltpu.make_async_copy(sky_hbm, sky, local_sem.at[0])
    obs_copy = pltpu.make_async_copy(obs_hbm.at[0], obs, local_sem.at[1])
    wt_copy = pltpu.make_async_copy(wt_hbm.at[0], wt, local_sem.at[2])
    small = [
        pltpu.make_async_copy(source, target, local_sem.at[4 + i])
        for i, (source, target) in enumerate(
            [
                (offsets_hbm, offsets), (owner_hbm, owner), (count_hbm, count),
                (rowk_hbm, rowk), (colk_hbm, colk), (cell_hbm, cell),
            ]
        )
    ]
    sky_copy.start()
    for copy in small:
        copy.start()
    obs_copy.start()
    wt_copy.start()

    barrier = pltpu.get_barrier_semaphore()

    def greet(d, carry):
        pl.semaphore_signal(
            barrier, inc=1, device_id={"facet": lax.rem(me + d, facets)},
            device_id_type=pl.DeviceIdType.MESH,
        )
        return carry

    lax.fori_loop(1, facets, greet, 0)
    for side in (left, right):
        pl.semaphore_signal(
            barrier, inc=1, device_id={"uv": side}, device_id_type=pl.DeviceIdType.MESH
        )

    def exchange(index, src, dst, side):
        return pltpu.make_async_remote_copy(
            src_ref=src, dst_ref=dst, send_sem=halo_send.at[index],
            recv_sem=halo_recv.at[index], device_id={"uv": side},
            device_id_type=pl.DeviceIdType.MESH,
        )

    half = facets // 2
    high, low = me // half, lax.rem(me, half)

    def peer(d):
        return lax.rem(high + d // half, 2) * half + lax.rem(low + d % half, half)

    def opposite(d):
        return d // half * half + (half - d % half) % half

    def send_contribution(d):
        return pltpu.make_async_remote_copy(
            src_ref=send1.at[d], dst_ref=recv1.at[me], send_sem=send_sem1.at[d],
            recv_sem=recv_sem1.at[opposite(d)], device_id={"facet": peer(d)},
            device_id_type=pl.DeviceIdType.MESH,
        )

    def take_contribution(d):
        return pltpu.make_async_remote_copy(
            src_ref=send1.at[d], dst_ref=recv1.at[peer(d)], send_sem=send_sem1.at[d],
            recv_sem=recv_sem1.at[d], device_id={"facet": peer(d)},
            device_id_type=pl.DeviceIdType.MESH,
        )

    def send_pieces(d):
        return pltpu.make_async_remote_copy(
            src_ref=send2.at[peer(d)], dst_ref=recv2.at[opposite(d)], send_sem=send_sem2.at[d],
            recv_sem=recv_sem2.at[opposite(d)], device_id={"facet": peer(d)},
            device_id_type=pl.DeviceIdType.MESH,
        )

    def take_pieces(d):
        return pltpu.make_async_remote_copy(
            src_ref=send2.at[peer(d)], dst_ref=recv2.at[d], send_sem=send_sem2.at[d],
            recv_sem=recv_sem2.at[d], device_id={"facet": peer(d)},
            device_id_type=pl.DeviceIdType.MESH,
        )

    order = list(range(half, facets)) + list(range(1, half))

    position = iota((1, strip), 1)
    taper[...] = sine((position.astype(F32) + 0.5) * (math.pi / strip)) * (1.0 / math.sqrt(strip))
    frequency = iota((LANES, XC), 1)
    first = (2 * me + 1) * (strip // facets)
    start = turn(frequency * (iota((LANES, XC), 0) + first), strip)
    step_cos, step_sin = turn(frequency[0:1] * LANES, strip)
    for copy in small:
        copy.wait()
    offset = jnp.zeros((slots, LANES), jnp.int32)
    slot_row = iota((slots, LANES), 0)
    for i in range(slots):
        offset = jnp.where(slot_row == i, offsets[owner[peer(i)]], offset)
    c, s = turn(offset * iota((slots, LANES), 1), strip)
    ahead_cos, ahead_sin = turn(offset * LANES, strip)
    for block in range(blocks):
        rows = slice(block * LANES, (block + 1) * LANES)
        shift[0, :, rows] = c
        shift[1, :, rows] = -s
        c, s = c * ahead_cos - s * ahead_sin, s * ahead_cos + c * ahead_sin
    sky_copy.wait()
    windowed[...] = (sky[...].astype(F32) * taper[...]).astype(BF16).astype(F32)
    def contribute(lowest, make_table):
        c, s = start
        total = jnp.zeros((half * columns, 2 * XC), F32)
        for group in range(blocks // GROUP):
            pieces = []
            for block in range(group * GROUP, (group + 1) * GROUP):
                if make_table:
                    left_part = jnp.concatenate([c, s], axis=0)
                    right_part = jnp.concatenate([-s, c], axis=0)
                    across[pl.ds(block * 2 * LANES, 2 * LANES)] = jnp.concatenate(
                        [left_part, right_part], axis=1
                    ).astype(BF16)
                    c, s = c * step_cos - s * step_sin, s * step_cos + c * step_sin
                rows = slice(block * LANES, (block + 1) * LANES)
                piece = windowed[:, rows]
                real, imag = shift[0, :, rows], shift[1, :, rows]
                pieces.append(
                    jnp.concatenate(
                        [
                            jnp.concatenate(
                                [real[i : i + 1] * piece, imag[i : i + 1] * piece], axis=1
                            ).astype(BF16)
                            for i in range(lowest, lowest + half)
                        ],
                        axis=0,
                    )
                )
            depth = GROUP * 2 * LANES
            total = total + jnp.dot(
                jnp.concatenate(pieces, axis=1), across[pl.ds(group * depth, depth)],
                preferred_element_type=F32,
            )
        send1[lowest : lowest + half] = total.astype(BF16).reshape(half, columns, 2 * XC)

    contribute(half, True)
    pl.semaphore_wait(barrier, facets + 1)
    for d in range(half, facets):
        send_contribution(d).start()
    contribute(0, False)
    for d in range(1, half):
        send_contribution(d).start()
    recv1[me] = send1[0]
    early = [
        exchange(0, obs_hbm.at[0, :, pl.ds(columns - 2 * EDGE, 2 * EDGE)], obs_halo.at[0], right),
        exchange(1, obs_hbm.at[0, :, pl.ds(0, 2 * EDGE)], obs_halo.at[1], left),
        exchange(2, wt_hbm.at[0, pl.ds(columns - EDGE, EDGE)], wt_halo.at[0], right),
        exchange(3, wt_hbm.at[0, pl.ds(0, EDGE)], wt_halo.at[1], left),
    ]
    for copy in early:
        copy.start()

    factor = 1.0 / math.sqrt(facets * XC)
    c, s = turn(iota((STEP, SG), 0) * iota((STEP, SG), 1), SG)
    c, s = c * factor, s * factor
    ahead_cos, ahead_sin = turn(iota((1, SG), 1) * STEP, SG)
    cosines, sines = [], []
    for _ in range(SG // STEP):
        cosines.append(c.astype(BF16))
        sines.append(s.astype(BF16))
        c, s = c * ahead_cos - s * ahead_sin, s * ahead_cos + c * ahead_sin
    fine_cos, fine_sin = jnp.concatenate(cosines, axis=0), jnp.concatenate(sines, axis=0)
    distance = iota((SG, live_slots), 0) - cell[...] + margin
    degrid = jnp.zeros((SG, live_slots), F32)
    for t in range(taps):
        degrid = jnp.where(distance == t, rowk[t], degrid)
    degrid = degrid.astype(BF16)
    grid_cos = jnp.dot(fine_cos, degrid, preferred_element_type=F32)
    grid_sin = jnp.dot(fine_sin, degrid, preferred_element_type=F32)
    grid[0:SG, 0:live_slots] = grid_cos.astype(BF16)
    grid[0:SG, live_slots:] = grid_sin.astype(BF16)
    grid[SG:, 0:live_slots] = (-grid_sin).astype(BF16)
    grid[SG:, live_slots:] = grid_cos.astype(BF16)

    for d in order:
        take_contribution(d).wait_recv()
    blank = jnp.zeros((columns, SG - XC), F32)
    sums = [jnp.zeros((columns, SG), F32), jnp.zeros((columns, SG), F32)]
    for f in range(facets):
        place = (2 * f + 1) * (SG // (2 * facets)) % SG
        arrived = recv1[f].astype(F32)
        for q in range(2):
            wide = jnp.concatenate([arrived[:, q * XC : (q + 1) * XC], blank], axis=1)
            sums[q] = sums[q] + pltpu.roll(wide, place, 1)
    z[...] = jnp.concatenate(sums, axis=1)
    late = [
        exchange(4, z.at[pl.ds(columns - EDGE, EDGE)], z_halo.at[0], right),
        exchange(5, z.at[pl.ds(0, EDGE)], z_halo.at[1], left),
    ]
    for copy in late:
        copy.start()

    degrid_back = jnp.transpose(degrid.astype(F32)).astype(BF16)
    grid_cos = jnp.dot(degrid_back, fine_cos, preferred_element_type=F32)
    grid_sin = jnp.dot(degrid_back, fine_sin, preferred_element_type=F32)
    back_table[0:live_slots, 0:SG] = grid_cos.astype(BF16)
    back_table[0:live_slots, SG:] = (-grid_sin).astype(BF16)
    back_table[live_slots:, 0:SG] = grid_sin.astype(BF16)
    back_table[live_slots:, SG:] = grid_cos.astype(BF16)


    obs_copy.wait()
    wt_copy.wait()
    for copy in early:
        copy.wait_recv()
    for copy in late:
        copy.wait_recv()
    rows = columns + 2 * EDGE
    before = jnp.where(band == 0, 0.0, z_halo[0])
    after = jnp.where(band == bands - 1, 0.0, z_halo[1])
    padded = jnp.concatenate([before, z[...], after], axis=0)
    convolved = jnp.zeros_like(padded)
    for t in range(taps):
        convolved = convolved + colk[t] * pltpu.roll(padded, (margin - t) % rows, 0)
    model = jnp.dot(convolved.astype(BF16), grid[...], preferred_element_type=F32)
    row = iota((rows, live_slots), 0)
    lowest = jnp.where(band == 0, EDGE, EDGE - margin)
    highest = jnp.where(band == bands - 1, EDGE + columns, EDGE + columns + margin)
    valid = (row >= lowest) & (row < highest) & (iota((rows, live_slots), 1) < count[0])
    weight = jnp.where(valid, jnp.concatenate([wt_halo[0], wt[...], wt_halo[1]], axis=0), 0.0)
    parts = []
    for p in range(2):
        seen = jnp.concatenate(
            [
                obs_halo[0, p].astype(F32)[EDGE:],
                obs[p].astype(F32),
                obs_halo[1, p].astype(F32)[:EDGE],
            ],
            axis=0,
        )
        parts.append(weight * (seen - model[:, p * live_slots : (p + 1) * live_slots]))
        residual[0, p] = parts[p][EDGE : EDGE + columns]
    rounded = jnp.concatenate(parts, axis=1).astype(BF16)
    gridded = jnp.dot(rounded, back_table[...], preferred_element_type=F32)
    back = jnp.zeros_like(gridded)
    for t in range(taps):
        back = back + colk[t] * pltpu.roll(gridded, (t - margin) % rows, 0)
    back = back[EDGE : EDGE + columns]
    for f in range(facets):
        place = (2 * f + 1) * (SG // (2 * facets)) % SG
        send2[f] = jnp.concatenate(
            [
                pltpu.roll(back[:, p * SG : (p + 1) * SG], (SG - place) % SG, 1)[:, :XC]
                for p in range(2)
            ],
            axis=1,
        ).astype(BF16)
    for d in order:
        send_pieces(d).start()
    recv2[0] = send2[me]

    c, s = jnp.transpose(start[0]), jnp.transpose(start[1])
    turn_cos = jnp.transpose(jnp.broadcast_to(step_cos, (LANES, XC)))
    turn_sin = jnp.transpose(jnp.broadcast_to(step_sin, (LANES, XC)))
    for block in range(blocks):
        upper = jnp.concatenate([c, s], axis=1)
        lower = jnp.concatenate([-s, c], axis=1)
        table[block] = jnp.concatenate([upper, lower], axis=0).astype(BF16)
        c, s = c * turn_cos - s * turn_sin, s * turn_cos + c * turn_sin

    for copy in early + late:
        copy.wait_send()
    for d in order:
        send_contribution(d).wait_send()
    for d in range(1, half):
        take_pieces(d).wait_recv()
    image_sum(recv2[0:half], 0, table, shift, partial, None, None)
    for d in range(half, facets):
        take_pieces(d).wait_recv()
    collected[...] = recv2[half:facets]
    for d in order:
        send_pieces(d).wait_send()


def image_kernel(
    residual, collected, partial, table, shift, taper, residual_hbm, dirty_hbm, dirty, sem
):
    groups = taper.shape[1] // LANES // GROUP
    residual_copy = pltpu.make_async_copy(residual, residual_hbm, sem.at[groups])
    residual_copy.start()
    copies = []

    def store(block):
        if (block + 1) % GROUP == 0:
            group = block // GROUP
            rows = pl.ds(group * GROUP * LANES, GROUP * LANES)
            copies.append(
                pltpu.make_async_copy(dirty.at[:, rows], dirty_hbm.at[:, rows], sem.at[group])
            )
            copies[-1].start()

    lowest = shift.shape[1] - collected.shape[0]
    image_sum(collected[...], lowest, table, shift, dirty, (partial, taper), store)
    for copy in copies:
        copy.wait()
    residual_copy.wait()


def pin(operand):
    return pltpu.with_memory_space_constraint(operand, pltpu.HBM)


def local(
    sky_image, subgrid_offsets, owner_order, visibility_count, visibility_cell, observed,
    visibility_weight, row_kernel, column_kernel,
):
    facets, bands = lax.axis_size("facet"), lax.axis_size("uv")
    columns, strip = sky_image.shape
    slots = facets
    live_slots = visibility_cell.shape[1]
    vmem = pl.BlockSpec(memory_space=pltpu.VMEM)
    hbm = pl.BlockSpec(memory_space=pltpu.HBM)
    dma = pltpu.SemaphoreType.DMA
    traded = pltpu.VMEM((facets, columns, 2 * XC), BF16)
    kept = pl.pallas_call(
        functools.partial(kernel, facets, bands),
        out_shape=(
            pltpu.VMEM(observed.shape, F32),
            pltpu.VMEM((facets - facets // 2, columns, 2 * XC), BF16),
            pltpu.VMEM((columns, strip), F32),
            pltpu.VMEM((strip // LANES, 2 * XC, 2 * LANES), BF16),
            pltpu.VMEM((2, slots, strip), F32),
            pltpu.VMEM((1, strip), F32),
        ),
        in_specs=[hbm] * 9,
        out_specs=(vmem,) * 6,
        scratch_shapes=[
            pltpu.SMEM(subgrid_offsets.shape, jnp.int32),
            pltpu.SMEM(owner_order.shape, jnp.int32),
            pltpu.SMEM(visibility_count.shape, jnp.int32),
            pltpu.SMEM(row_kernel.shape, F32),
            pltpu.SMEM(column_kernel.shape, F32),
            pltpu.VMEM(visibility_cell.shape, jnp.int32),
            pltpu.VMEM((columns, strip), BF16),
            pltpu.VMEM((2, columns, live_slots), BF16),
            pltpu.VMEM((columns, live_slots), F32),
            pltpu.VMEM((2, 2, 2 * EDGE, live_slots), BF16),
            pltpu.VMEM((2, EDGE, live_slots), F32),
            pltpu.VMEM((columns, strip), F32),
            pltpu.VMEM((2 * strip, 2 * XC), BF16),
            traded,
            traded,
            pltpu.VMEM((2 * SG, 2 * live_slots), BF16),
            pltpu.VMEM((2 * live_slots, 2 * SG), BF16),
            pltpu.VMEM((columns, 2 * SG), F32),
            pltpu.VMEM((2, EDGE, 2 * SG), F32),
            traded,
            traded,
            dma((10,)),
            dma((facets,)),
            dma((facets,)),
            dma((facets,)),
            dma((facets,)),
            dma((6,)),
            dma((6,)),
        ],
        compiler_params=pltpu.CompilerParams(
            collective_id=0, has_side_effects=True, vmem_limit_bytes=32 * 1024 * 1024
        ),
    )(
        pin(subgrid_offsets), pin(owner_order), visibility_count, pin(row_kernel),
        pin(column_kernel), pin(visibility_cell), pin(sky_image), pin(observed),
        pin(visibility_weight),
    )
    return pl.pallas_call(
        image_kernel,
        out_shape=(
            jax.ShapeDtypeStruct(observed.shape, F32),
            jax.ShapeDtypeStruct(sky_image.shape, F32),
        ),
        in_specs=[vmem] * 6,
        out_specs=(hbm, hbm),
        scratch_shapes=[
            pltpu.VMEM((columns, strip), F32),
            dma((strip // LANES // GROUP + 1,)),
        ],
        compiler_params=pltpu.CompilerParams(vmem_limit_bytes=32 * 1024 * 1024),
    )(*kept)


def solution(mesh):
    in_specs = (
        P("uv", "facet"), P(), P(), P("facet"), P("facet", None), P("facet", None, "uv", None),
        P("facet", "uv", None), P(), P(),
    )
    out_specs = (P("facet", None, "uv", None), P("uv", "facet"))
    return jax.shard_map(local, mesh=mesh, in_specs=in_specs, out_specs=out_specs, check_vma=False)
```
